32 devices in a mesh: dp: 4 (over y, x), expert: 8 (over z, core).
Axes of the slice: x: 2, y: 2, z: 4, core: 2. Of those that a mesh axis runs over, the one named last changes fastest.
Arguments:
- tokens: bfloat16 [4096, 1024], P(('dp', 'expert')), may hold values from -6 to 6
- routes: int32 [4096, 8], P(('dp', 'expert')), may hold values from 0 to 15, all different within a row; in each aligned block of 128 rows (0 to 127, 128 to 255, ...) at most 96 rows name the same one
- gates: float32 [4096, 8], P(('dp', 'expert')), may hold values from 0.05 to 0.5
- cotangent: bfloat16 [4096, 1024], P(('dp', 'expert')), may hold values from -6 to 6
- partner: int32 [16], replicated, may hold values from 0 to 15, as said below
- w_gate_up: bfloat16 [16, 1024, 768], P('expert'), may hold values from -0.1875 to 0.1875
- w_down: bfloat16 [16, 1024, 384], P('expert'), may hold values from -0.3125 to 0.3125
Outputs:
- mixed: bfloat16 [4096, 1024], P(('dp', 'expert'))
- grad_tokens: bfloat16 [4096, 1024], P(('dp', 'expert'))
- grad_gate_up: float32 [16, 1024, 768], P('expert', 'dp')
- grad_down: float32 [16, 1024, 384], P('expert', 'dp')
The draws below stay inside these ranges and needn't reach their ends.
Inputs may be any that keep to these rules, and one draw needn't show every extreme that they name: `routes`: A token names 8 different experts. In each device's block of 128 consecutive tokens no expert is named by more than 96 tokens, a bound that some block reaches. partner is a permutation that is its own inverse: each slot either keeps its expert or trades it with one slot of the device half the expert axis away (slot s lies on index s // 2 of the expert axis); each device trades at most one of its slots, and some slots trade in every draw.
All inputs are finite; a program needn't handle non-finite values.
Results may differ from the reference program's by a relative error of at most 0.01.
Values may be sent and summed in bfloat16 or wider, within the bound.
No kernel may reach another device: no remote copies, remote signals or barrier semaphores. Data moves between devices by JAX's collectives and lax.ppermute only.
A program may use at most 128 MiB of HBM per device.

```python
import math
import jax
import jax.numpy as jnp
import numpy as np
from jax import lax

D = 1024
FF = 384
TOP = 8
EXP_DEV = 2
TOK_DEV = 128
EXPERTS = 16
CAP = 96
TOKENS = 4096
N_DP = 4
N_EXPERT = 8


def draw_partner(key, part):
    half_dev = EXPERTS // (2 * EXP_DEV)
    key_flag = jax.random.fold_in(key, 11)
    key_low = jax.random.fold_in(key, 12)
    key_high = jax.random.fold_in(key, 13)
    flags = jax.random.randint(key_flag, (half_dev,), 0, 2, dtype=jnp.int32)
    flags = flags.at[0].set(1)
    low_pick = jax.random.randint(key_low, (half_dev,), 0, EXP_DEV, dtype=jnp.int32)
    high_pick = jax.random.randint(key_high, (half_dev,), 0, EXP_DEV, dtype=jnp.int32)
    devices = jnp.arange(half_dev, dtype=jnp.int32)
    low_slot = devices * EXP_DEV + low_pick
    high_slot = (devices + half_dev) * EXP_DEV + high_pick
    result = jnp.arange(EXPERTS, dtype=jnp.int32)
    result = result.at[low_slot].set(jnp.where(flags == 1, high_slot, low_slot))
    result = result.at[high_slot].set(jnp.where(flags == 1, low_slot, high_slot))
    return result


def block_scale(key, dims, split, smallest, high):
    factor_of = 1.0
    for dim, parts in split:
        heights = jax.random.uniform(jax.random.fold_in(jax.random.fold_in(key, 6), dim), (parts,), jnp.float32, smallest / len(split), high / len(split))
        factor_of = factor_of * jnp.repeat(jnp.exp(heights), dims[dim] // parts).reshape((-1,) + (1,) * (len(dims) - 1 - dim))
    return factor_of


def shared_out(rng, own, number, rows, amount, top, reach, skew):
    sequence = jax.random.permutation(rng, amount)
    heavy_load, ordinary = portions_of(amount, rows * top, reach, skew, True), portions_of(amount, rows * top, reach, skew, False)
    places = jnp.arange(amount)

    def named(tallies, turn):
        used = int((tallies > 0).sum())
        fixed = max(1, used // 4)
        passed = fixed + (places - fixed + turn * (used - fixed)) % max(1, amount - fixed)
        return jnp.zeros((amount,), jnp.int32).at[sequence[jnp.where(places < fixed, places, passed)]].set(jnp.asarray(tallies, jnp.int32))

    tallies = jnp.where(number % 4 == 0, named(heavy_load, number // 4), named(ordinary, number - number // 4 - 1))
    mixed = jax.random.permutation(jax.random.fold_in(own, 3), amount)
    giver, taker = mixed[0:amount // 2 * 2:2], mixed[1:amount // 2 * 2:2]
    slack = jnp.minimum(tallies[giver] - 1, reach - tallies[taker]) // 2
    slack = jnp.where((giver == sequence[0]) | (taker == sequence[0]) | (tallies[taker] == 0), 0, jnp.maximum(slack, 0))
    passed = jax.random.randint(jax.random.fold_in(own, 4), (amount // 2,), 0, 1 << 20) % (slack + 1)
    tallies = tallies.at[giver].add(-passed).at[taker].add(passed)
    labels = jnp.searchsorted(jnp.cumsum(tallies), jnp.arange(rows * top), side="right").astype(jnp.int32)
    listing = labels.reshape(top, rows).T
    listing = listing[jax.random.permutation(jax.random.fold_in(own, 1), rows)]
    turn = jax.random.randint(jax.random.fold_in(own, 2), (rows, 1), 0, top)
    return jnp.take_along_axis(listing, (jnp.arange(top)[None, :] + turn) % top, axis=1)


def portions_of(number_of, total, bound, skew, full):
    weights = [(1 << 20) // math.isqrt(rank ** skew) + 1 for rank in range(1, number_of + 1)]
    largest = bound if full else min(bound, max(-(-total // number_of), total * weights[0] // sum(weights)))
    least = 1 if total - largest >= number_of - 1 else 0
    given, surplus = [largest] + [least] * (number_of - 1), total - largest - least * (number_of - 1)
    while surplus > 0:
        free = [i for i in range(1, number_of) if given[i] < largest] or [i for i in range(1, number_of) if given[i] < bound]
        mass, budget = sum([weights[i] for i in free]), surplus
        for i in free:
            addition = min(bound - given[i], max(1, budget * weights[i] // mass), surplus)
            given[i] = given[i] + addition
            surplus = surplus - addition
    return np.array(given)


def normal_values(own_key, extent, spread, limit, shards=(), kind=jnp.bfloat16):
    values = jax.random.normal(own_key, extent, jnp.float32) * spread
    if len(shards) > 0:
        values = block_scale(own_key, extent, shards, -0.22, 0.18) * values
    return jnp.clip(values, min=-limit, max=limit).astype(kind)


def setup_inputs(seed: int = 0) -> dict:
    seeds = jax.random.split(jax.random.key(seed), 8)
    tokens = normal_values(seeds[0], (TOKENS, D), 1.0, 6.0, ((0, 32),))
    routes_keys = jax.random.split(jax.random.fold_in(seeds[1], 1), TOKENS // TOK_DEV)
    routes_turns = jax.random.permutation(jax.random.fold_in(seeds[1], 3), TOKENS // TOK_DEV)
    routes = jax.vmap(lambda own, number: shared_out(jax.random.fold_in(seeds[1], 2), own, number, TOK_DEV, EXPERTS, TOP, CAP, 2))(routes_keys, routes_turns).reshape((TOKENS, TOP))
    gates = jnp.clip(0.05 + 0.45 * jax.random.uniform(seeds[2], (TOKENS, TOP), jnp.float32) ** block_scale(seeds[2], (TOKENS, TOP), ((0, 32),), -0.2, 0.2), 0.05, 0.5)
    cotangent = normal_values(seeds[3], (TOKENS, D), 1.0, 6.0, ((0, 32),))
    partner = draw_partner(jax.random.fold_in(seeds[7], 71), 0)
    w_gate_up = normal_values(seeds[5], (EXPERTS, D, 2 * FF), D ** -0.5, 0.1875, ((0, 8),))
    w_down = normal_values(seeds[6], (EXPERTS, D, FF), FF ** -0.5, 0.3125, ((0, 8),))
    return {"tokens": tokens, "routes": routes, "gates": gates, "cotangent": cotangent, "partner": partner, "w_gate_up": w_gate_up, "w_down": w_down}


grad_scale = 0.0625


def reference(tokens, routes, gates, cotangent, partner, w_gate_up, w_down):
    assign_total = TOKENS * TOP
    most_rows = N_DP * N_EXPERT * CAP
    flat = routes.reshape(-1).astype(jnp.int32)
    order = jnp.argsort(flat, stable=True).astype(jnp.int32)
    sorted_keys = flat[order]
    counts = jnp.zeros((EXPERTS,), jnp.int32).at[flat].add(1)
    starts = (jnp.cumsum(counts) - counts).astype(jnp.int32)
    ranked = jnp.arange(assign_total, dtype=jnp.int32) - starts[sorted_keys]
    table = jnp.full((EXPERTS, most_rows), assign_total, jnp.int32).at[sorted_keys, ranked].set(order)
    token_pad = jnp.concatenate([tokens, jnp.zeros((1, D), tokens.dtype)], axis=0)
    cot_pad = jnp.concatenate([cotangent, jnp.zeros((1, D), cotangent.dtype)], axis=0)
    gate_pad = jnp.concatenate([gates.reshape(-1), jnp.zeros((1,), gates.dtype)], axis=0)
    highest = lax.Precision.HIGHEST

    def one_expert(carry, inputs):
        mixed_sum, grad_sum = carry
        index, weight_gu, weight_dn = inputs
        token_index = (index // TOP).astype(jnp.int32)
        rows = token_pad[token_index].astype(jnp.float32)
        gate_rows = gate_pad[index].astype(jnp.float32)
        wgu_full = weight_gu.astype(jnp.float32)
        wdn_full = weight_dn.astype(jnp.float32)
        pre_act = jnp.dot(rows, wgu_full, preferred_element_type=jnp.float32, precision=highest)
        gate_pre = pre_act[:, :FF]
        up_pre = pre_act[:, FF:]
        sigmoid_gate = jax.nn.sigmoid(gate_pre)
        silu_gate = gate_pre * sigmoid_gate
        hidden = (silu_gate * up_pre).astype(jnp.bfloat16)
        expert_out = jnp.dot(hidden.astype(jnp.float32), wdn_full.T, preferred_element_type=jnp.float32, precision=highest).astype(jnp.bfloat16)
        mixed_sum = mixed_sum.at[token_index].add(gate_rows[:, None] * expert_out.astype(jnp.float32))
        grad_out = (gate_rows[:, None] * cot_pad[token_index].astype(jnp.float32)).astype(jnp.bfloat16)
        grad_out_full = grad_out.astype(jnp.float32)
        grad_hidden = jnp.dot(grad_out_full, wdn_full, preferred_element_type=jnp.float32, precision=highest)
        grad_down = jnp.dot(grad_out_full.T, hidden.astype(jnp.float32), preferred_element_type=jnp.float32, precision=highest)
        grad_gate = grad_hidden * up_pre * sigmoid_gate * (1.0 + gate_pre * (1.0 - sigmoid_gate))
        grad_up = grad_hidden * silu_gate
        grad_pre = jnp.concatenate([grad_gate, grad_up], axis=-1).astype(jnp.bfloat16)
        grad_pre_full = grad_pre.astype(jnp.float32)
        grad_rows = jnp.dot(grad_pre_full, wgu_full.T, preferred_element_type=jnp.float32, precision=highest).astype(jnp.bfloat16)
        grad_sum = grad_sum.at[token_index].add(grad_rows.astype(jnp.float32))
        grad_gu = jnp.dot(rows.T, grad_pre_full, preferred_element_type=jnp.float32, precision=highest)
        stacked = jnp.concatenate([grad_gu, grad_down], axis=-1) * grad_scale
        return (mixed_sum, grad_sum), stacked

    start = (jnp.zeros((TOKENS + 1, D), jnp.float32), jnp.zeros((TOKENS + 1, D), jnp.float32))
    (mixed_sum, grad_sum), expert_grad = lax.scan(one_expert, start, (table, w_gate_up, w_down))
    mixed = mixed_sum[:TOKENS].astype(jnp.bfloat16)
    grad_tokens = grad_sum[:TOKENS].astype(jnp.bfloat16)
    by_slot = jnp.take(expert_grad, partner.astype(jnp.int32), axis=0)
    return mixed, grad_tokens, by_slot[:, :, :2 * FF], by_slot[:, :, 2 * FF:]
```

```python
import jax
import jax.numpy as jnp
from jax import lax
from jax.sharding import PartitionSpec as P

grad_scale = 0.0625


def partner_2(block, axis, distance):
    count = lax.axis_size(axis)
    route = []
    for low in range(count):
        high = low | 1 << distance
        if high != low and high < count:
            route += [(low, high), (high, low)]
    return lax.ppermute(block, axis, route)


def table_lookup(table, keys):
    hits = keys[..., None] == jnp.arange(table.shape[0], dtype=jnp.int32)
    return jnp.sum(jnp.where(hits, table, 0), axis=-1)


def pick_slots(own_slots, received, moved, source_local):
    slots = own_slots.shape[0]
    index = jnp.where(moved, slots + source_local, jnp.arange(slots, dtype=jnp.int32))
    stacked = jnp.concatenate([own_slots, received], axis=0)
    return jnp.take(stacked, index, axis=0)


def routed(tokens, routes, gates, cotangent, partner, w_gate_up, w_down):
    count_tokens, top_k = routes.shape
    width = tokens.shape[1]
    hidden_units = w_down.shape[2]
    n_expert = lax.axis_size("expert")
    exp_slots = w_gate_up.shape[0]
    experts_all = n_expert * exp_slots
    capacity = 3 * count_tokens * top_k // (2 * experts_all)
    pair_bit = n_expert.bit_length() - 2
    my_index = lax.axis_index("expert")
    slot_ids = my_index * exp_slots + jnp.arange(exp_slots, dtype=jnp.int32)
    partner_of = table_lookup(partner, slot_ids)
    moved = partner_of // exp_slots != my_index
    source_local = partner_of % exp_slots
    packed = jnp.concatenate([w_gate_up, w_down], axis=-1)
    target = table_lookup(partner, routes)
    received = partner_2(packed, "expert", pair_bit)
    packed = pick_slots(packed, received, moved, source_local)
    weight_gu = packed[:, :, : 2 * hidden_units]
    weight_dn = packed[:, :, 2 * hidden_units :]
    assign_total = count_tokens * top_k
    flat_slots = target.reshape(-1)
    hits = (flat_slots[:, None] == jnp.arange(experts_all, dtype=jnp.int32)).astype(jnp.int32)
    ranked = jnp.sum(jnp.cumsum(hits, axis=0) * hits, axis=1) - 1
    position = flat_slots * capacity + ranked
    filler = (
        jnp.full((experts_all * capacity,), assign_total, jnp.int32)
        .at[position]
        .set(jnp.arange(assign_total, dtype=jnp.int32))
    )
    buffer_shape = (n_expert, exp_slots, capacity, width)
    token_pad = jnp.concatenate([tokens, jnp.zeros((1, width), tokens.dtype)], axis=0)
    sending_rows = token_pad[filler // top_k].reshape(buffer_shape)
    arrived = lax.all_to_all(sending_rows, "expert", split_axis=0, concat_axis=0, tiled=True)
    pre_act = jnp.einsum("sjcd,jdf->sjcf", arrived, weight_gu, preferred_element_type=jnp.float32)
    gate_pre = pre_act[..., :hidden_units]
    up_pre = pre_act[..., hidden_units:]
    sigmoid_gate = jax.nn.sigmoid(gate_pre)
    silu_gate = gate_pre * sigmoid_gate
    hidden = (silu_gate * up_pre).astype(jnp.bfloat16)
    expert_out = jnp.einsum(
        "sjcf,jdf->sjcd", hidden, weight_dn, preferred_element_type=jnp.float32
    ).astype(jnp.bfloat16)
    returned = lax.all_to_all(expert_out, "expert", split_axis=0, concat_axis=0, tiled=True)
    picked = returned.reshape(-1, width)[position].reshape(count_tokens, top_k, width)
    mixed = jnp.einsum("tk,tkd->td", gates, picked.astype(jnp.float32)).astype(jnp.bfloat16)
    grad_out = (
        (gates[:, :, None] * cotangent[:, None, :].astype(jnp.float32))
        .astype(jnp.bfloat16)
        .reshape(assign_total, width)
    )
    grad_pad = jnp.concatenate([grad_out, jnp.zeros((1, width), jnp.bfloat16)], axis=0)
    grad_arrived = lax.all_to_all(
        grad_pad[filler].reshape(buffer_shape), "expert", split_axis=0, concat_axis=0, tiled=True
    )
    grad_hidden = jnp.einsum(
        "sjcd,jdf->sjcf", grad_arrived, weight_dn, preferred_element_type=jnp.float32
    )
    grad_down = jnp.einsum(
        "sjcf,sjcd->jdf", hidden, grad_arrived, preferred_element_type=jnp.float32
    )
    grad_gate = grad_hidden * up_pre * sigmoid_gate * (1.0 + gate_pre * (1.0 - sigmoid_gate))
    grad_up = grad_hidden * silu_gate
    grad_pre = jnp.concatenate([grad_gate, grad_up], axis=-1).astype(jnp.bfloat16)
    grad_rows = jnp.einsum(
        "sjcf,jdf->sjcd", grad_pre, weight_gu, preferred_element_type=jnp.float32
    ).astype(jnp.bfloat16)
    grad_gu = jnp.einsum("sjcd,sjcf->jdf", arrived, grad_pre, preferred_element_type=jnp.float32)
    grad_back = lax.all_to_all(grad_rows, "expert", split_axis=0, concat_axis=0, tiled=True)
    gathered = grad_back.reshape(-1, width)[position].reshape(count_tokens, top_k, width)
    grad_tokens = jnp.sum(gathered.astype(jnp.float32), axis=1).astype(jnp.bfloat16)
    terms = jnp.concatenate([grad_gu, grad_down], axis=-1) * grad_scale
    reduced = lax.psum_scatter(terms, "dp", scatter_dimension=1, tiled=True)
    return (
        mixed,
        grad_tokens,
        reduced[:, :, : 2 * hidden_units],
        reduced[:, :, 2 * hidden_units :],
    )


def swap_with(block, axis, mask):
    return lax.ppermute(block, axis, [(i, i ^ mask) for i in range(lax.axis_size(axis))])


def gather_relative(block):
    n_expert = lax.axis_size("expert")
    column = [block] + [swap_with(block, "expert", mask) for mask in range(2, n_expert, 2)]
    column = jnp.stack(column)
    return jnp.stack([column, swap_with(column, "expert", 1)], axis=1).reshape(-1, block.shape[-1])


def reduce_relative(partial, count_tokens):
    n_expert = lax.axis_size("expert")
    terms = partial.reshape(n_expert // 2, 2, count_tokens, -1)
    other = swap_with(terms[:, 1].astype(jnp.bfloat16), "expert", 1)
    pair = terms[:, 0].astype(jnp.float32) + other.astype(jnp.float32)
    total = pair[0]
    for step in range(1, n_expert // 2):
        sent = swap_with(pair[step].astype(jnp.bfloat16), "expert", 2 * step)
        total = total + sent.astype(jnp.float32)
    return total.astype(jnp.bfloat16)


def relative(array, index):
    count = array.shape[0]
    for bit in range(count.bit_length() - 1):
        parts = array.reshape((count >> bit + 1, 2, 1 << bit) + array.shape[1:])
        array = jnp.where((index >> bit) & 1 == 1, parts[:, ::-1], parts).reshape(array.shape)
    return array


def scatter_sum(terms):
    me = lax.axis_index("dp")
    low = me & 1
    high = me >> 1
    by = terms.reshape((2, 2) + terms.shape[1:])
    pick = lambda array, axis, at: lax.dynamic_index_in_dim(array, at, axis, keepdims=False)
    first, second = by[:, :, 0], by[:, :, 1]
    f32 = jnp.float32
    got_low = swap_with(pick(first, 1, 1 - low), "dp", 1)
    got_high = swap_with(pick(second, 0, 1 - high), "dp", 2)
    pair_low = pick(first, 1, low).astype(f32) + got_low.astype(f32)
    pair_high = pick(second, 0, high).astype(f32) + got_high.astype(f32)
    end_low = swap_with(pick(pair_low, 0, 1 - high).astype(jnp.bfloat16), "dp", 2)
    end_high = swap_with(pick(pair_high, 0, 1 - low).astype(jnp.bfloat16), "dp", 1)
    sum_low = pick(pair_low, 0, high) + end_low.astype(f32)
    sum_high = pick(pair_high, 0, low) + end_high.astype(f32)
    return jnp.concatenate([sum_low, sum_high], axis=0)


def dense(tokens, routes, gates, cotangent, partner, w_gate_up, w_down):
    count_tokens, _ = routes.shape
    width = tokens.shape[1]
    units = w_down.shape[2]
    n_expert = lax.axis_size("expert")
    n_dp = lax.axis_size("dp")
    experts_all = n_expert * 2
    bf16, f32 = jnp.bfloat16, jnp.float32
    me = lax.axis_index("expert")
    partner_of = table_lookup(partner, me * 2 + jnp.arange(2, dtype=jnp.int32))
    moved = partner_of // 2 != me
    flip = moved[1]

    slot_gates = jnp.sum(
        jnp.where(
            routes[None] == jnp.arange(experts_all, dtype=jnp.int32)[:, None, None], gates[None], 0.0
        ),
        axis=-1,
    )
    all_gates = lax.all_to_all(
        slot_gates.reshape(n_expert, 2, count_tokens), "expert", 0, 0, tiled=True
    )
    all_gates = relative(all_gates, me)
    all_gates = jnp.where(flip, all_gates[:, ::-1], all_gates)
    gate_of = [all_gates[:, i].reshape(-1, 1) for i in range(2)]

    rows = gather_relative(tokens)
    cots = gather_relative(cotangent)
    ordered = lambda w: jnp.concatenate(
        [jnp.where(flip, w[1], w[0]), jnp.where(flip, w[0], w[1])], axis=1
    )
    up = ordered(w_gate_up)
    down = ordered(w_down)

    pre_act = jnp.dot(rows, up, preferred_element_type=f32)
    weighted, factors = [], []
    for i in range(2):
        gate_pre = pre_act[:, 2 * i * units : (2 * i + 1) * units]
        up_pre = pre_act[:, (2 * i + 1) * units : (2 * i + 2) * units]
        sigmoid_gate = jax.nn.sigmoid(gate_pre)
        silu_gate = gate_pre * sigmoid_gate
        weighted.append((gate_of[i] * silu_gate * up_pre).astype(bf16))
        factors.append(
            gate_of[i] * up_pre * sigmoid_gate * (1.0 + gate_pre * (1.0 - sigmoid_gate))
        )
        factors.append(gate_of[i] * silu_gate)
    weighted = jnp.concatenate(weighted, axis=1)
    contract = lambda a, b, i, j: lax.dot_general(
        a, b, (((i,), (j,)), ((), ())), preferred_element_type=f32
    )
    mixed_part = contract(weighted, down, 1, 1)
    mixed = reduce_relative(mixed_part, count_tokens)

    back = jnp.dot(cots, down, preferred_element_type=f32)
    grad_pre = [
        (back[:, i // 2 * units : (i // 2 + 1) * units] * factors[i]).astype(bf16) for i in range(4)
    ]
    sums = []
    for i in range(2):
        grad_gu = contract(rows, jnp.concatenate(grad_pre[2 * i : 2 * i + 2], axis=1), 0, 0)
        grad_dn = contract(cots, weighted[:, i * units : (i + 1) * units], 0, 0)
        terms = jnp.concatenate([grad_gu, grad_dn], axis=1).astype(bf16)
        terms = terms.reshape(n_dp, 2, width // (2 * n_dp), 3 * units)
        sums.append(scatter_sum(terms) * grad_scale)
    traded = swap_with(sums[0].astype(bf16), "expert", n_expert // 2).astype(f32)
    lead = jnp.where(moved[0] | moved[1], traded, sums[0])
    out = jnp.where(flip, jnp.stack([sums[1], lead]), jnp.stack([lead, sums[1]]))

    grad_part = contract(jnp.concatenate(grad_pre, axis=1), up, 1, 1)
    grad_tokens = reduce_relative(grad_part, count_tokens)
    return mixed, grad_tokens, out[:, :, : 2 * units], out[:, :, 2 * units :]


def local(tokens, routes, gates, cotangent, partner, w_gate_up, w_down):
    count_tokens, top_k = routes.shape
    slots = w_gate_up.shape[0]
    experts_all = lax.axis_size("expert") * slots
    few = experts_all <= 4 * top_k and slots == 2 and lax.axis_size("dp") == 4
    step = dense if few else routed
    return step(tokens, routes, gates, cotangent, partner, w_gate_up, w_down)


def solution(mesh):
    in_specs = (
        P(("dp", "expert"), None),
        P(("dp", "expert"), None),
        P(("dp", "expert"), None),
        P(("dp", "expert"), None),
        P(),
        P("expert", None, None),
        P("expert", None, None),
    )
    out_specs = (
        P(("dp", "expert"), None),
        P(("dp", "expert"), None),
        P("expert", "dp", None),
        P("expert", "dp", None),
    )
    return jax.shard_map(local, mesh=mesh, in_specs=in_specs, out_specs=out_specs, check_vma=False)
```

```python
import functools

import jax
import jax.numpy as jnp
from jax import lax
from jax.experimental import pallas as pl
from jax.experimental.pallas import tpu as pltpu
from jax.sharding import PartitionSpec as P

grad_scale = 0.0625
vmem = 20 << 20


def partner_2(block, axis, distance):
    count = lax.axis_size(axis)
    route = []
    for low in range(count):
        high = low | 1 << distance
        if high != low and high < count:
            route += [(low, high), (high, low)]
    return lax.ppermute(block, axis, route)


def table_lookup(table, keys):
    hits = keys[..., None] == jnp.arange(table.shape[0], dtype=jnp.int32)
    return jnp.sum(jnp.where(hits, table, 0), axis=-1)


def pick_slots(own_slots, received, moved, source_local):
    slots = own_slots.shape[0]
    index = jnp.where(moved, slots + source_local, jnp.arange(slots, dtype=jnp.int32))
    stacked = jnp.concatenate([own_slots, received], axis=0)
    return jnp.take(stacked, index, axis=0)


def routed(tokens, routes, gates, cotangent, partner, w_gate_up, w_down):
    count_tokens, top_k = routes.shape
    width = tokens.shape[1]
    hidden_units = w_down.shape[2]
    n_expert = lax.axis_size("expert")
    exp_slots = w_gate_up.shape[0]
    experts_all = n_expert * exp_slots
    capacity = 3 * count_tokens * top_k // (2 * experts_all)
    pair_bit = n_expert.bit_length() - 2
    my_index = lax.axis_index("expert")
    slot_ids = my_index * exp_slots + jnp.arange(exp_slots, dtype=jnp.int32)
    partner_of = table_lookup(partner, slot_ids)
    moved = partner_of // exp_slots != my_index
    source_local = partner_of % exp_slots
    packed = jnp.concatenate([w_gate_up, w_down], axis=-1)
    target = table_lookup(partner, routes)
    received = partner_2(packed, "expert", pair_bit)
    packed = pick_slots(packed, received, moved, source_local)
    weight_gu = packed[:, :, : 2 * hidden_units]
    weight_dn = packed[:, :, 2 * hidden_units :]
    assign_total = count_tokens * top_k
    flat_slots = target.reshape(-1)
    hits = (flat_slots[:, None] == jnp.arange(experts_all, dtype=jnp.int32)).astype(jnp.int32)
    ranked = jnp.sum(jnp.cumsum(hits, axis=0) * hits, axis=1) - 1
    position = flat_slots * capacity + ranked
    filler = (
        jnp.full((experts_all * capacity,), assign_total, jnp.int32)
        .at[position]
        .set(jnp.arange(assign_total, dtype=jnp.int32))
    )
    buffer_shape = (n_expert, exp_slots, capacity, width)
    token_pad = jnp.concatenate([tokens, jnp.zeros((1, width), tokens.dtype)], axis=0)
    sending_rows = token_pad[filler // top_k].reshape(buffer_shape)
    arrived = lax.all_to_all(sending_rows, "expert", split_axis=0, concat_axis=0, tiled=True)
    pre_act = jnp.einsum("sjcd,jdf->sjcf", arrived, weight_gu, preferred_element_type=jnp.float32)
    gate_pre = pre_act[..., :hidden_units]
    up_pre = pre_act[..., hidden_units:]
    sigmoid_gate = jax.nn.sigmoid(gate_pre)
    silu_gate = gate_pre * sigmoid_gate
    hidden = (silu_gate * up_pre).astype(jnp.bfloat16)
    expert_out = jnp.einsum(
        "sjcf,jdf->sjcd", hidden, weight_dn, preferred_element_type=jnp.float32
    ).astype(jnp.bfloat16)
    returned = lax.all_to_all(expert_out, "expert", split_axis=0, concat_axis=0, tiled=True)
    picked = returned.reshape(-1, width)[position].reshape(count_tokens, top_k, width)
    mixed = jnp.einsum("tk,tkd->td", gates, picked.astype(jnp.float32)).astype(jnp.bfloat16)
    grad_out = (
        (gates[:, :, None] * cotangent[:, None, :].astype(jnp.float32))
        .astype(jnp.bfloat16)
        .reshape(assign_total, width)
    )
    grad_pad = jnp.concatenate([grad_out, jnp.zeros((1, width), jnp.bfloat16)], axis=0)
    grad_arrived = lax.all_to_all(
        grad_pad[filler].reshape(buffer_shape), "expert", split_axis=0, concat_axis=0, tiled=True
    )
    grad_hidden = jnp.einsum(
        "sjcd,jdf->sjcf", grad_arrived, weight_dn, preferred_element_type=jnp.float32
    )
    grad_down = jnp.einsum(
        "sjcf,sjcd->jdf", hidden, grad_arrived, preferred_element_type=jnp.float32
    )
    grad_gate = grad_hidden * up_pre * sigmoid_gate * (1.0 + gate_pre * (1.0 - sigmoid_gate))
    grad_up = grad_hidden * silu_gate
    grad_pre = jnp.concatenate([grad_gate, grad_up], axis=-1).astype(jnp.bfloat16)
    grad_rows = jnp.einsum(
        "sjcf,jdf->sjcd", grad_pre, weight_gu, preferred_element_type=jnp.float32
    ).astype(jnp.bfloat16)
    grad_gu = jnp.einsum("sjcd,sjcf->jdf", arrived, grad_pre, preferred_element_type=jnp.float32)
    grad_back = lax.all_to_all(grad_rows, "expert", split_axis=0, concat_axis=0, tiled=True)
    gathered = grad_back.reshape(-1, width)[position].reshape(count_tokens, top_k, width)
    grad_tokens = jnp.sum(gathered.astype(jnp.float32), axis=1).astype(jnp.bfloat16)
    terms = jnp.concatenate([grad_gu, grad_down], axis=-1) * grad_scale
    reduced = lax.psum_scatter(terms, "dp", scatter_dimension=1, tiled=True)
    return (
        mixed,
        grad_tokens,
        reduced[:, :, : 2 * hidden_units],
        reduced[:, :, 2 * hidden_units :],
    )


def swap_with(block, axis, mask):
    return lax.ppermute(block, axis, [(i, i ^ mask) for i in range(lax.axis_size(axis))])


def send(block, pairs):
    return lax.ppermute(block, "expert", [(2 * a + c, 2 * b + c) for a, b in pairs for c in range(2)])


def after(value, *earlier):
    return lax.optimization_barrier((value,) + earlier)[0]


def near_blocks(block, inner):
    two = swap_with(block, "expert", 4)
    one = swap_with(block, "expert", 2)
    middle = send(block, [(1, 2), (2, 1)])
    ends = send(two, [(1, 0), (2, 3)])
    return [block, one, two, jnp.where(inner, middle, ends)]


def direct_blocks(block):
    return [block] + [swap_with(block, "expert", mask) for mask in (2, 4, 6)]


def both_cores(blocks):
    return [(block, swap_with(block, "expert", 1)) for block in blocks]


def reduce_relative(kept, other):
    f32, bf16 = jnp.float32, jnp.bfloat16
    pair = [(kept[k].astype(f32) + other[k].astype(f32)) for k in range(4)]
    far = pair[3].astype(bf16)
    passed = send(far, [(0, 1), (3, 2)])
    one = swap_with(pair[1].astype(bf16), "expert", 2)
    middle = send(far, [(1, 2), (2, 1)])
    two = swap_with((pair[2] + passed.astype(f32)).astype(bf16), "expert", 4)
    total = pair[0] + one.astype(f32) + middle.astype(f32) + two.astype(f32)
    return total.astype(bf16), passed


def relative(array, index):
    count = array.shape[0]
    for bit in range(count.bit_length() - 1):
        parts = array.reshape((count >> bit + 1, 2, 1 << bit) + array.shape[1:])
        array = jnp.where((index >> bit) & 1 == 1, parts[:, ::-1], parts).reshape(array.shape)
    return array


def contract(a, b, i, j):
    return lax.dot_general(a, b, (((i,), (j,)), ((), ())), preferred_element_type=jnp.float32)


def message_kernel(tokens_ref, routes_ref, gates_ref, out_ref, *, experts):
    rows, width = tokens_ref.shape
    lanes = out_ref.shape[1] - width
    out_ref[:, :width] = tokens_ref[...]
    lane = lax.broadcasted_iota(jnp.int32, (rows, lanes), 1)
    expert = lane % experts
    gate = jnp.zeros((rows, lanes), jnp.float32)
    for k in range(routes_ref.shape[1]):
        gate = gate + jnp.where(routes_ref[:, k : k + 1] == expert, gates_ref[:, k : k + 1], 0.0)
    high = gate.astype(jnp.bfloat16).astype(jnp.float32)
    middle = (gate - high).astype(jnp.bfloat16).astype(jnp.float32)
    low = gate - high - middle
    third = lane // experts
    value = jnp.where(third == 0, high, jnp.where(third == 1, middle, jnp.where(third == 2, low, 0.0)))
    out_ref[:, width:] = value.astype(out_ref.dtype)


def message(tokens, routes, gates, experts):
    rows, width = tokens.shape
    return pl.pallas_call(
        functools.partial(message_kernel, experts=experts),
        out_shape=jax.ShapeDtypeStruct((rows, width + 128), tokens.dtype),
        cost_estimate=pl.CostEstimate(flops=0, bytes_accessed=1 << 20, transcendentals=0),
        name="message",
    )(tokens, routes, gates)


def gate_of(ref, width, expert, experts):
    values = ref[:, width:].astype(jnp.float32)
    lane = lax.broadcasted_iota(jnp.int32, values.shape, 1)
    chosen = jnp.logical_and(lane % experts == expert, lane < 3 * experts)
    return jnp.sum(jnp.where(chosen, values, 0.0), axis=1, keepdims=True)


def forward_kernel(at, x_ref, y_ref, up_ref, down_ref, h_ref, f_ref, kept_ref, sent_ref, *, experts):
    units = down_ref.shape[2]
    half = kept_ref.shape[0]
    width = up_ref.shape[1]
    x = jnp.concatenate([x_ref[:, :width], y_ref[:, :width]], axis=0)
    total = None
    for i in range(2):
        slot = jnp.bitwise_xor(at[1], i)
        pre = jnp.dot(x, up_ref[slot], preferred_element_type=jnp.float32)
        gate_pre, up_pre = pre[:, :units], pre[:, units:]
        expert = 2 * at[2] + slot
        gate = [gate_of(ref, width, expert, experts) for ref in (x_ref, y_ref)]
        gate = jnp.concatenate(gate, axis=0)
        sig = 0.5 * jnp.tanh(0.5 * gate_pre) + 0.5
        scaled = gate * sig
        silu = scaled * gate_pre
        hidden = (silu * up_pre).astype(jnp.bfloat16)
        h_ref[i] = hidden
        f_ref[i, :, :units] = (up_pre * (scaled + silu * (1.0 - sig))).astype(f_ref.dtype)
        f_ref[i, :, units:] = silu.astype(f_ref.dtype)
        part = contract(hidden, down_ref[slot], 1, 1)
        total = part if total is None else total + part
    kept_ref[...] = total[:half].astype(kept_ref.dtype)
    sent_ref[...] = total[half:].astype(sent_ref.dtype)


def call(kernel, name, scalars, operands, outs, flops, places=None, scratch=()):
    places = places or [pltpu.VMEM] * len(outs)
    return pl.pallas_call(
        kernel,
        in_specs=[pl.BlockSpec(memory_space=pltpu.SMEM)]
        + [pl.BlockSpec(memory_space=pltpu.VMEM)] * len(operands),
        out_specs=[pl.BlockSpec(memory_space=place) for place in places],
        scratch_shapes=list(scratch),
        out_shape=[jax.ShapeDtypeStruct(shape, dtype) for shape, dtype in outs],
        compiler_params=pltpu.CompilerParams(vmem_limit_bytes=vmem),
        cost_estimate=pl.CostEstimate(flops=2 * flops, bytes_accessed=0, transcendentals=0),
        name=name,
    )(scalars, *operands)


def forward(at, pair, w_gate_up, w_down, experts):
    count_tokens = pair[0].shape[0]
    width = w_gate_up.shape[1]
    n = 2 * count_tokens
    units = w_down.shape[2]
    bf16 = jnp.bfloat16
    outs = [((2, n, units), bf16), ((2, n, 2 * units), bf16)] + [((count_tokens, width), bf16)] * 2
    kernel = functools.partial(forward_kernel, experts=experts)
    flops = 12 * n * width * units
    return call(kernel, "forward", at, (*pair, w_gate_up, w_down), outs, flops)


def weight_kernel(at, *refs):
    xs, cs, fs, hs = refs[:8], refs[8:16], refs[16:20], refs[20:24]
    down_ref, *outs = refs[24:35]
    held, sems = refs[35:41], refs[41]
    copies = [
        pltpu.make_async_copy(source, target, sems.at[i])
        for i, (source, target) in enumerate(zip(held, (outs[0], *outs[5:])))
    ]
    outs = [held[0], *outs[1:5], *held[1:]]
    units = down_ref.shape[2]
    block = xs[0].shape[0]
    for order in range(2):
        p_ref, send_a, send_b, keep_a, keep_b = outs[5 * order : 5 * order + 5]
        rows = send_a.shape[1]
        down = down_ref[jnp.bitwise_xor(at[1], order)]
        for k in range(4):
            c = jnp.concatenate([cs[2 * k][...], cs[2 * k + 1][...]], axis=0)
            back = jnp.dot(c, down, preferred_element_type=jnp.float32)
            here = slice(2 * k * block, 2 * (k + 1) * block)
            factor = fs[k][order].astype(jnp.float32)
            p_ref[here, :units] = (back * factor[:, :units]).astype(p_ref.dtype)
            p_ref[here, units:] = (back * factor[:, units:]).astype(p_ref.dtype)
        for i in range(4):
            start = pl.multiple_of(jnp.bitwise_xor(at[0], i) * 2 * rows, 2 * rows)
            column = pl.ds(start, 2 * rows)
            x = jnp.concatenate([ref[:, column] for ref in xs], axis=0)
            c = jnp.concatenate([ref[:, column] for ref in cs], axis=0)
            h = jnp.concatenate([ref[order] for ref in hs], axis=0)
            first = (contract(x, p_ref[...], 0, 0) * grad_scale).astype(send_a.dtype)
            last = (contract(c, h, 0, 0) * grad_scale).astype(send_a.dtype)
            ref_a = send_a if i & 1 else keep_a
            ref_b = send_b if i & 2 else keep_b
            ref_a[i >> 1, :, : 2 * units] = first[:rows]
            ref_a[i >> 1, :, 2 * units :] = last[:rows]
            ref_b[i & 1, :, : 2 * units] = first[rows:]
            ref_b[i & 1, :, 2 * units :] = last[rows:]
        for copy in copies[:1] if order == 0 else copies[1:]:
            copy.start()
    for copy in copies:
        copy.wait()


def weight_terms(at, rows, cots, factors, hidden, w_down):
    count_tokens, width = cots[0][0].shape
    n = 8 * count_tokens
    units = w_down.shape[2]
    bf16 = jnp.bfloat16
    flat = lambda pairs: [block for pair in pairs for block in pair]
    outs = [((n, 2 * units), bf16)] + [((2, width // 8, 3 * units), bf16)] * 4
    operands = (*flat(rows), *flat(cots), *factors, *hidden, w_down)
    flops = 16 * n * width * units
    far = [outs[0], *outs]
    scratch = [pltpu.VMEM(*out) for out in far] + [pltpu.SemaphoreType.DMA((len(far),))]
    places = [pltpu.HBM] + [pltpu.VMEM] * 4 + [pltpu.HBM] * 5
    result = call(weight_kernel, "weight_terms", at, operands, outs * 2, flops, places, scratch)
    return result[:5], result[5:]


def backward_kernel(at, p_ref, q_ref, up_ref, kept_ref, sent_ref):
    half = kept_ref.shape[1]
    for k in range(kept_ref.shape[0]):
        here = slice(2 * k * half, 2 * (k + 1) * half)
        total = contract(p_ref[here], up_ref[at[1]], 1, 1)
        total = total + contract(q_ref[here], up_ref[1 - at[1]], 1, 1)
        kept_ref[k] = total[:half].astype(kept_ref.dtype)
        sent_ref[k] = total[half:].astype(sent_ref.dtype)


def backward(at, first, second, w_gate_up, count_tokens):
    width = w_gate_up.shape[1]
    outs = [((first.shape[0] // (2 * count_tokens), count_tokens, width), jnp.bfloat16)] * 2
    flops = 4 * first.size * width
    return call(backward_kernel, "backward", at, (first, second, w_gate_up), outs, flops)


def finish_kernel(at, a0, a1, b0, b1, ta, tb, gu_ref, dn_ref):
    columns = gu_ref.shape[2]
    rows = a0.shape[0]
    for h, (own, other, traded) in enumerate(((a0, a1, ta), (b0, b1, tb))):
        lead = jnp.where(at[1] == 1, traded[...].astype(jnp.float32), own[...])
        for slot, value in ((at[0], lead), (1 - at[0], other[...])):
            gu_ref[slot, h * rows : (h + 1) * rows, :] = value[:, :columns]
            dn_ref[slot, h * rows : (h + 1) * rows, :] = value[:, columns:]


def finish(at, sums, traded, units):
    rows = traded[0].shape[0]
    full = pl.BlockSpec(memory_space=pltpu.VMEM)
    return pl.pallas_call(
        finish_kernel,
        in_specs=[pl.BlockSpec(memory_space=pltpu.SMEM)] + [full] * 6,
        out_specs=[full, full],
        out_shape=[
            jax.ShapeDtypeStruct((2, 2 * rows, 2 * units), jnp.float32),
            jax.ShapeDtypeStruct((2, 2 * rows, units), jnp.float32),
        ],
        compiler_params=pltpu.CompilerParams(vmem_limit_bytes=vmem),
        cost_estimate=pl.CostEstimate(flops=0, bytes_accessed=0, transcendentals=0),
        name="finish",
    )(at, sums[0][0], sums[1][0], sums[0][1], sums[1][1], traded[0], traded[1])


def pair_sum(send_a, send_b, keep_a, keep_b):
    f32 = jnp.float32
    got_a = swap_with(send_a, "dp", 1)
    got_b = swap_with(send_b, "dp", 2)
    return keep_a.astype(f32) + got_a.astype(f32), keep_b.astype(f32) + got_b.astype(f32)


def quarter_sum(pair_a, pair_b):
    f32, bf16 = jnp.float32, jnp.bfloat16
    end_a = swap_with(pair_a[1].astype(bf16), "dp", 2)
    end_b = swap_with(pair_b[1].astype(bf16), "dp", 1)
    return pair_a[0] + end_a.astype(f32), pair_b[0] + end_b.astype(f32)


def dense(tokens, routes, gates, cotangent, partner, w_gate_up, w_down):
    count_tokens, _ = routes.shape
    units = w_down.shape[2]
    n_expert = lax.axis_size("expert")
    bf16, f32, i32 = jnp.bfloat16, jnp.float32, jnp.int32
    me = lax.axis_index("expert")
    partner_of = table_lookup(partner, me * 2 + jnp.arange(2, dtype=i32))
    moved = partner_of // 2 != me
    flip = moved[1].astype(i32)
    trades = jnp.any(moved).astype(i32)
    inner = (me // 2 == 1) | (me // 2 == 2)

    line = near_blocks(message(tokens, routes, gates, 2 * n_expert), inner)
    rows = both_cores(line)
    cots = both_cores(direct_blocks(after(cotangent, line[0])))

    at = jnp.stack([lax.axis_index("dp"), flip, me])
    passes = [forward(at, rows[k], w_gate_up, w_down, 2 * n_expert) for k in range(4)]
    hidden, factors, kept, sent = zip(*passes)

    (first, *terms), (second, *later) = weight_terms(at, rows, cots, factors, hidden, w_down)
    pair = pair_sum(*terms)
    other = [swap_with(block, "expert", 1) for block in sent]
    mixed, passed = reduce_relative(kept, other)
    sums = [quarter_sum(*pair)]
    later[:2] = after(later[:2], *pair)
    second = after(second, passed)
    kept, sent = backward(at, first, second, w_gate_up, count_tokens)
    sums.append(quarter_sum(*pair_sum(*later)))
    grad_tokens, _ = reduce_relative(kept, swap_with(sent, "expert", 1))
    traded = [swap_with(half.astype(bf16), "expert", n_expert // 2) for half in sums[0]]
    grad_gu, grad_dn = finish(jnp.stack([flip, trades]), sums, traded, units)
    return mixed, grad_tokens, grad_gu, grad_dn


def local(tokens, routes, gates, cotangent, partner, w_gate_up, w_down):
    count_tokens, top_k = routes.shape
    slots = w_gate_up.shape[0]
    experts_all = lax.axis_size("expert") * slots
    line = lax.axis_size("dp") == 4 and lax.axis_size("expert") == 8
    few = experts_all <= 4 * top_k and slots == 2
    step = dense if few and line else routed
    return step(tokens, routes, gates, cotangent, partner, w_gate_up, w_down)


def solution(mesh):
    in_specs = (
        P(("dp", "expert"), None),
        P(("dp", "expert"), None),
        P(("dp", "expert"), None),
        P(("dp", "expert"), None),
        P(),
        P("expert", None, None),
        P("expert", None, None),
    )
    out_specs = (
        P(("dp", "expert"), None),
        P(("dp", "expert"), None),
        P("expert", "dp", None),
        P("expert", "dp", None),
    )
    return jax.shard_map(local, mesh=mesh, in_specs=in_specs, out_specs=out_specs, check_vma=False)
```

```python
import functools

import jax
import jax.numpy as jnp
from jax import lax
from jax.experimental import pallas as pl
from jax.experimental.pallas import tpu as pltpu
from jax.sharding import PartitionSpec as P

grad_scale = 0.0625
vmem = 12 << 20


def partner_2(block, axis, distance):
    count = lax.axis_size(axis)
    route = []
    for low in range(count):
        high = low | 1 << distance
        if high != low and high < count:
            route += [(low, high), (high, low)]
    return lax.ppermute(block, axis, route)


def table_lookup(table, keys):
    hits = keys[..., None] == jnp.arange(table.shape[0], dtype=jnp.int32)
    return jnp.sum(jnp.where(hits, table, 0), axis=-1)


def pick_slots(own_slots, received, moved, source_local):
    slots = own_slots.shape[0]
    index = jnp.where(moved, slots + source_local, jnp.arange(slots, dtype=jnp.int32))
    stacked = jnp.concatenate([own_slots, received], axis=0)
    return jnp.take(stacked, index, axis=0)


def routed(tokens, routes, gates, cotangent, partner, w_gate_up, w_down):
    count_tokens, top_k = routes.shape
    width = tokens.shape[1]
    hidden_units = w_down.shape[2]
    n_expert = lax.axis_size("expert")
    exp_slots = w_gate_up.shape[0]
    experts_all = n_expert * exp_slots
    capacity = 3 * count_tokens * top_k // (2 * experts_all)
    pair_bit = n_expert.bit_length() - 2
    my_index = lax.axis_index("expert")
    slot_ids = my_index * exp_slots + jnp.arange(exp_slots, dtype=jnp.int32)
    partner_of = table_lookup(partner, slot_ids)
    moved = partner_of // exp_slots != my_index
    source_local = partner_of % exp_slots
    packed = jnp.concatenate([w_gate_up, w_down], axis=-1)
    target = table_lookup(partner, routes)
    received = partner_2(packed, "expert", pair_bit)
    packed = pick_slots(packed, received, moved, source_local)
    weight_gu = packed[:, :, : 2 * hidden_units]
    weight_dn = packed[:, :, 2 * hidden_units :]
    assign_total = count_tokens * top_k
    flat_slots = target.reshape(-1)
    hits = (flat_slots[:, None] == jnp.arange(experts_all, dtype=jnp.int32)).astype(jnp.int32)
    ranked = jnp.sum(jnp.cumsum(hits, axis=0) * hits, axis=1) - 1
    position = flat_slots * capacity + ranked
    filler = (
        jnp.full((experts_all * capacity,), assign_total, jnp.int32)
        .at[position]
        .set(jnp.arange(assign_total, dtype=jnp.int32))
    )
    buffer_shape = (n_expert, exp_slots, capacity, width)
    token_pad = jnp.concatenate([tokens, jnp.zeros((1, width), tokens.dtype)], axis=0)
    sending_rows = token_pad[filler // top_k].reshape(buffer_shape)
    arrived = lax.all_to_all(sending_rows, "expert", split_axis=0, concat_axis=0, tiled=True)
    pre_act = jnp.einsum("sjcd,jdf->sjcf", arrived, weight_gu, preferred_element_type=jnp.float32)
    gate_pre = pre_act[..., :hidden_units]
    up_pre = pre_act[..., hidden_units:]
    sigmoid_gate = jax.nn.sigmoid(gate_pre)
    silu_gate = gate_pre * sigmoid_gate
    hidden = (silu_gate * up_pre).astype(jnp.bfloat16)
    expert_out = jnp.einsum(
        "sjcf,jdf->sjcd", hidden, weight_dn, preferred_element_type=jnp.float32
    ).astype(jnp.bfloat16)
    returned = lax.all_to_all(expert_out, "expert", split_axis=0, concat_axis=0, tiled=True)
    picked = returned.reshape(-1, width)[position].reshape(count_tokens, top_k, width)
    mixed = jnp.einsum("tk,tkd->td", gates, picked.astype(jnp.float32)).astype(jnp.bfloat16)
    grad_out = (
        (gates[:, :, None] * cotangent[:, None, :].astype(jnp.float32))
        .astype(jnp.bfloat16)
        .reshape(assign_total, width)
    )
    grad_pad = jnp.concatenate([grad_out, jnp.zeros((1, width), jnp.bfloat16)], axis=0)
    grad_arrived = lax.all_to_all(
        grad_pad[filler].reshape(buffer_shape), "expert", split_axis=0, concat_axis=0, tiled=True
    )
    grad_hidden = jnp.einsum(
        "sjcd,jdf->sjcf", grad_arrived, weight_dn, preferred_element_type=jnp.float32
    )
    grad_down = jnp.einsum(
        "sjcf,sjcd->jdf", hidden, grad_arrived, preferred_element_type=jnp.float32
    )
    grad_gate = grad_hidden * up_pre * sigmoid_gate * (1.0 + gate_pre * (1.0 - sigmoid_gate))
    grad_up = grad_hidden * silu_gate
    grad_pre = jnp.concatenate([grad_gate, grad_up], axis=-1).astype(jnp.bfloat16)
    grad_rows = jnp.einsum(
        "sjcf,jdf->sjcd", grad_pre, weight_gu, preferred_element_type=jnp.float32
    ).astype(jnp.bfloat16)
    grad_gu = jnp.einsum("sjcd,sjcf->jdf", arrived, grad_pre, preferred_element_type=jnp.float32)
    grad_back = lax.all_to_all(grad_rows, "expert", split_axis=0, concat_axis=0, tiled=True)
    gathered = grad_back.reshape(-1, width)[position].reshape(count_tokens, top_k, width)
    grad_tokens = jnp.sum(gathered.astype(jnp.float32), axis=1).astype(jnp.bfloat16)
    terms = jnp.concatenate([grad_gu, grad_down], axis=-1) * grad_scale
    reduced = lax.psum_scatter(terms, "dp", scatter_dimension=1, tiled=True)
    return (
        mixed,
        grad_tokens,
        reduced[:, :, : 2 * hidden_units],
        reduced[:, :, 2 * hidden_units :],
    )


def swap_with(block, axis, mask):
    return lax.ppermute(block, axis, [(i, i ^ mask) for i in range(lax.axis_size(axis))])


def send(block, pairs):
    return lax.ppermute(block, "expert", [(2 * a + c, 2 * b + c) for a, b in pairs for c in range(2)])


def both_cores(block):
    return block, swap_with(block, "expert", 1)


def contract(a, b, i, j):
    return lax.dot_general(a, b, (((i,), (j,)), ((), ())), preferred_element_type=jnp.float32)


def message_kernel(tokens_ref, cotangent_ref, routes_ref, gates_ref, out_ref, again_ref, *, experts):
    rows, width = tokens_ref.shape
    lanes = out_ref.shape[1] - 2 * width
    out_ref[:, :width] = tokens_ref[...]
    out_ref[:, width : 2 * width] = cotangent_ref[...]
    lane = lax.broadcasted_iota(jnp.int32, (rows, lanes), 1)
    expert = lane % experts
    gate = jnp.zeros((rows, lanes), jnp.float32)
    routes, gates = routes_ref[...].T, gates_ref[...].T
    for k in range(routes.shape[1]):
        gate = gate + jnp.where(routes[:, k : k + 1] == expert, gates[:, k : k + 1], 0.0)
    high = gate.astype(jnp.bfloat16).astype(jnp.float32)
    middle = (gate - high).astype(jnp.bfloat16).astype(jnp.float32)
    low = gate - high - middle
    third = lane // experts
    value = jnp.where(third == 0, high, jnp.where(third == 1, middle, jnp.where(third == 2, low, 0.0)))
    out_ref[:, 2 * width :] = value.astype(out_ref.dtype)
    again_ref[...] = out_ref[...]


def message(tokens, cotangent, routes, gates, experts):
    rows, width = tokens.shape
    return pl.pallas_call(
        functools.partial(message_kernel, experts=experts),
        out_shape=[jax.ShapeDtypeStruct((n, 2 * width + 128), tokens.dtype) for n in (rows, rows)],
        cost_estimate=pl.CostEstimate(flops=0, bytes_accessed=1 << 20, transcendentals=0),
        name="message",
    )(tokens, cotangent, routes.T, gates.T)


def gate_of(ref, width, expert, experts):
    values = ref[:, 2 * width :].astype(jnp.float32)
    lane = lax.broadcasted_iota(jnp.int32, values.shape, 1)
    chosen = jnp.logical_and(lane % experts == expert, lane < 3 * experts)
    return jnp.sum(jnp.where(chosen, values, 0.0), axis=1, keepdims=True)


def marked(kernel, count, *refs):
    refs[count - 1][...] = jnp.zeros_like(refs[count - 1])
    kernel(*refs[: count - 1], *refs[count:])


def call(kernel, name, scalars, operands, outs, flops, places=None, scratch=()):
    outs = [*outs, ((8, 128), jnp.float32)]
    places = [*(places or [pltpu.VMEM] * (len(outs) - 1)), pltpu.VMEM]
    return pl.pallas_call(
        functools.partial(marked, kernel, 1 + len(operands) + len(outs)),
        in_specs=[pl.BlockSpec(memory_space=pltpu.SMEM)]
        + [pl.BlockSpec(memory_space=pltpu.VMEM)] * len(operands),
        out_specs=[pl.BlockSpec(memory_space=place) for place in places],
        out_shape=[jax.ShapeDtypeStruct(shape, dtype) for shape, dtype in outs],
        scratch_shapes=list(scratch),
        compiler_params=pltpu.CompilerParams(vmem_limit_bytes=vmem),
        cost_estimate=pl.CostEstimate(flops=int(flops), bytes_accessed=0, transcendentals=0),
        name=name,
    )(scalars, *operands)


def hold_kernel(*refs):
    del refs


def hold(values, *earlier):
    anywhere = pl.BlockSpec(memory_space=pl.ANY)
    n = len(values)
    return pl.pallas_call(
        hold_kernel,
        in_specs=[anywhere] * (n + len(earlier)),
        out_specs=[anywhere] * n,
        out_shape=[jax.ShapeDtypeStruct(x.shape, x.dtype) for x in values],
        input_output_aliases={i: i for i in range(n)},
        compiler_params=pltpu.CompilerParams(vmem_limit_bytes=vmem),
        cost_estimate=pl.CostEstimate(flops=0, bytes_accessed=0, transcendentals=0),
        name="hold",
    )(*values, *earlier)


def inner_kernel(at, xs, up_ref, down_ref, h_ref, p_ref, experts):
    width, units = up_ref.shape[1], down_ref.shape[2]
    x = jnp.concatenate([ref[:, :width] for ref in xs], axis=0)
    c = jnp.concatenate([ref[:, width : 2 * width] for ref in xs], axis=0)
    for i in range(2):
        slot = jnp.bitwise_xor(at[1], i)
        pre = jnp.dot(x, up_ref[slot], preferred_element_type=jnp.float32)
        back = jnp.dot(c, down_ref[slot], preferred_element_type=jnp.float32)
        gate_pre, up_pre = pre[:, :units], pre[:, units:]
        expert = 2 * at[2] + slot
        gate = [gate_of(ref, width, expert, experts) for ref in xs]
        gate = jnp.concatenate(gate, axis=0)
        sig = 0.5 * jnp.tanh(0.5 * gate_pre) + 0.5
        scaled = gate * sig
        silu = scaled * gate_pre
        h_ref[i] = (silu * up_pre).astype(h_ref.dtype)
        p_ref[i, :, :units] = (back * up_pre * (scaled + silu * (1.0 - sig))).astype(p_ref.dtype)
        p_ref[i, :, units:] = (back * silu).astype(p_ref.dtype)


def outer_kernel(at, h_ref, p_ref, up_ref, down_ref, *outs):
    kept_ref, sent_ref = outs[-2:]
    width = up_ref.shape[1]
    half = kept_ref.shape[0]
    slots = [jnp.bitwise_xor(at[1], i) for i in range(2)]
    out = sum(contract(h_ref[i], down_ref[slots[i]], 1, 1) for i in range(2))
    kept_ref[:, :width] = out[:half].astype(kept_ref.dtype)
    sent_ref[:, :width] = out[half:].astype(sent_ref.dtype)
    out = sum(contract(p_ref[i], up_ref[slots[i]], 1, 1) for i in range(2))
    kept_ref[:, width:] = out[:half].astype(kept_ref.dtype)
    sent_ref[:, width:] = out[half:].astype(sent_ref.dtype)


def near_kernel(at, *refs, pieces, experts):
    xs, (up_ref, down_ref, h_ref, p_ref, kept_ref, sent_ref) = refs[:pieces], refs[pieces:]
    inner_kernel(at, xs, up_ref, down_ref, h_ref, p_ref, experts)
    outer_kernel(at, h_ref, p_ref, up_ref, down_ref, kept_ref, sent_ref)


def far_kernel(at, *refs, pieces, experts):
    inner_kernel(at, refs[:pieces], *refs[pieces:], experts)


def term(xs, ps, hs, order, column, width):
    units = hs[0].shape[2]
    x = jnp.concatenate([ref[:, pl.ds(column, width // 4)] for ref in xs], axis=0)
    c = jnp.concatenate([ref[:, pl.ds(width + column, width // 4)] for ref in xs], axis=0)
    p = jnp.concatenate([ref[order] for ref in ps], axis=0)
    h = jnp.concatenate([ref[order] for ref in hs], axis=0)
    return contract(x, p, 0, 0), contract(c, h, 0, 0)


def early_kernel(at, *refs, pieces):
    xs, ps, hs, outs = refs[:pieces], refs[pieces : pieces + 3], refs[pieces + 3 : pieces + 6], refs[pieces + 6 :]
    units = hs[0].shape[2]
    quarter = outs[0].shape[1]
    for order in range(2):
        for i in range(4):
            column = pl.multiple_of(jnp.bitwise_xor(at[0], i) * quarter, quarter)
            first, last = term(xs, ps, hs, order, column, 4 * quarter)
            outs[order][i, :, : 2 * units] = first.astype(outs[order].dtype)
            outs[order][i, :, 2 * units :] = last.astype(outs[order].dtype)


def late_kernel(at, *refs, pieces, order):
    xs, (p_ref, h_ref, sum_ref), outs = refs[:pieces], refs[pieces : pieces + 3], refs[-4:]
    send_a, send_b, keep_a, keep_b = outs
    units = h_ref.shape[2]
    quarter = sum_ref.shape[1]
    rows = quarter // 2
    for i in (1, 3, 2, 0):
        column = pl.multiple_of(jnp.bitwise_xor(at[0], i) * quarter, quarter)
        first, last = term(xs, (p_ref,), (h_ref,), order, column, 4 * quarter)
        first = ((first + sum_ref[i, :, : 2 * units]) * grad_scale).astype(send_a.dtype)
        last = ((last + sum_ref[i, :, 2 * units :]) * grad_scale).astype(send_a.dtype)
        ref_a = send_a if i & 1 else keep_a
        ref_b = send_b if i & 2 else keep_b
        ref_a[i >> 1, :, : 2 * units] = first[:rows]
        ref_a[i >> 1, :, 2 * units :] = last[:rows]
        ref_b[i & 1, :, : 2 * units] = first[rows:]
        ref_b[i & 1, :, 2 * units :] = last[rows:]


def far_block_kernel(at, middle, ends, *refs):
    refs[-1][...] = jnp.where(at[4] == 1, middle[...], ends[...])


def line_kernel(at, kept, other, *outs):
    out = outs[-1]
    out[...] = (kept[...].astype(jnp.float32) + other[...].astype(jnp.float32)).astype(out.dtype)


def pair_kernel(at, got_a, got_b, keep_a, keep_b, *refs):
    f32 = jnp.float32
    more, results = refs[: (len(refs) - 3) * 5 // 7], refs[-2:]
    end_a, end_b, own = refs[len(more) : len(more) + 3]
    for half, (got, keep, out) in enumerate(((got_a, keep_a, end_a), (got_b, keep_b, end_b))):
        out[...] = (keep[1].astype(f32) + got[1].astype(f32)).astype(out.dtype)
        own[half] = keep[0].astype(f32) + got[0].astype(f32)
    if more:
        value = sum(ref[...].astype(f32) for ref in more).astype(results[0].dtype)
        for i, ref in enumerate(results):
            ref[...] = value[:, i * ref.shape[1] : (i + 1) * ref.shape[1]]


def lead_kernel(at, end_a, end_b, own, done, sent_a, sent_b, first):
    del done
    for half, (end, sent) in enumerate(((end_a, sent_a), (end_b, sent_b))):
        value = own[half] + end[...].astype(jnp.float32)
        first[half] = value
        sent[...] = value.astype(sent.dtype)


def finish_kernel(at, first, second, end_a, end_b, traded_a, traded_b, gu_ref, dn_ref):
    columns = gu_ref.shape[2]
    rows = end_a.shape[0]
    for half, (end, traded) in enumerate(((end_a, traded_a), (end_b, traded_b))):
        here = slice(half * rows, (half + 1) * rows)
        lead = jnp.where(at[3] == 1, traded[...].astype(jnp.float32), first[half])
        for slot, value in ((at[1], lead), (1 - at[1], second[half] + end[...].astype(jnp.float32))):
            gu_ref[slot, here, :] = value[:, :columns]
            dn_ref[slot, here, :] = value[:, columns:]


def dense(tokens, routes, gates, cotangent, partner, w_gate_up, w_down):
    count_tokens, _ = routes.shape
    units = w_down.shape[2]
    n_expert = lax.axis_size("expert")
    bf16, f32, i32 = jnp.bfloat16, jnp.float32, jnp.int32
    me = lax.axis_index("expert")
    partner_of = table_lookup(partner, me * 2 + jnp.arange(2, dtype=i32))
    moved = partner_of // 2 != me
    flip = moved[1].astype(i32)
    trades = jnp.any(moved).astype(i32)
    inner = (me // 2 == 1) | (me // 2 == 2)

    experts = 2 * n_expert
    width = tokens.shape[1]
    n = 2 * count_tokens
    at = jnp.stack([lax.axis_index("dp"), flip, me, trades, inner.astype(i32)])
    flops = 4 * n * width * units
    weights = (w_gate_up, w_down)
    inner_outs = [((2, n, units), bf16), ((2, n, 2 * units), bf16)]
    outer_outs = [((count_tokens, 2 * width), bf16)] * 2

    rows, columns = width // 8, 3 * units
    part = [((2, rows, columns), bf16)] * 4
    one_block = ((rows, columns), bf16)
    both = ((2, rows, columns), f32)

    block, again = message(tokens, cotangent, routes, gates, experts)
    two = swap_with(block, "expert", 4)
    one = swap_with(block, "expert", 2)

    def near(pieces, cost):
        kernel = functools.partial(near_kernel, pieces=len(pieces), experts=experts)
        outs = inner_outs + outer_outs
        return call(kernel, "near_block", at, (*pieces, *weights), outs, cost * flops)

    ends = send(two, [(1, 0), (2, 3)])
    (again,) = hold([again], two)
    middle = send(again, [(1, 2), (2, 1)])
    pieces = [both_cores(block)]
    passes = [near(pieces[0], 12)]
    (one,) = hold([one], passes[0][4])
    pieces += [both_cores(one), both_cores(two)]
    passes += [near(pieces[1], 12), near(pieces[2], 15)]
    hidden, grads, kept, sent, _ = map(list, zip(*passes))
    flat = [piece for block in pieces for piece in block]
    *sums, done = call(
        functools.partial(early_kernel, pieces=len(flat)),
        "early_terms",
        at,
        (*flat, *grads, *hidden),
        [((4, width // 4, 3 * units), f32)] * 2,
        27 * flops,
    )
    other = [swap_with(block, "expert", 1) for block in sent]

    def line(k, *earlier):
        operands = (kept[k], other[k], *earlier)
        going, done = call(line_kernel, "line_terms", at, operands, outer_outs[:1], 0)
        return swap_with(going, "expert", 2 * k), done

    (got_one, mark_one), (got_two, mark_two) = line(1), line(2)

    far, _ = call(far_block_kernel, "far_block", at, (middle, ends, done, mark_one, mark_two), [(block.shape, bf16)], 0)
    far = both_cores(far)
    kernel = functools.partial(far_kernel, pieces=2, experts=experts)
    h, p, _ = call(kernel, "far_hidden", at, (*far, *weights), inner_outs, 12 * flops)

    def late(i, *earlier):
        kernel = functools.partial(late_kernel, pieces=2, order=i)
        return call(kernel, "late_terms", at, (*far, p, h, sums[i], *earlier), part, 6 * flops)

    def halves(send_a, send_b, keep_a, keep_b, more):
        got_a, got_b = swap_with(send_a, "dp", 1), swap_with(send_b, "dp", 2)
        operands = (got_a, got_b, keep_a, keep_b, *more)
        outs = [one_block, one_block, both] + [((count_tokens, width), bf16)] * (2 if more else 0)
        end_a, end_b, own, *results, _ = call(pair_kernel, "pair_terms", at, operands, outs, 0)
        return swap_with(end_a, "dp", 2), swap_with(end_b, "dp", 1), own, results

    *first, done = late(0)
    *second, done = late(1, done)
    k, s, _ = call(outer_kernel, "far_results", at, (h, p, *weights, done), outer_outs, 12 * flops)
    kept.append(k)
    other.append(swap_with(s, "expert", 1))
    got_three, done = line(3, got_one, got_two)
    end_a, end_b, own, _ = halves(*first, [])
    *leading, head, _ = call(
        lead_kernel, "lead_terms", at, (end_a, end_b, own, done), [one_block, one_block, both], 0
    )
    traded = [swap_with(half, "expert", n_expert // 2) for half in leading]
    more = [kept[0], other[0], got_one, got_two, got_three]
    end_a, end_b, tail, (mixed, grad_tokens) = halves(*second, more)
    grad_gu, grad_dn, _ = call(
        finish_kernel,
        "finish",
        at,
        (head, tail, end_a, end_b, *traded),
        [((2, 2 * rows, 2 * units), f32), ((2, 2 * rows, units), f32)],
        0,
    )
    return mixed, grad_tokens, grad_gu, grad_dn


def local(tokens, routes, gates, cotangent, partner, w_gate_up, w_down):
    count_tokens, top_k = routes.shape
    slots = w_gate_up.shape[0]
    experts_all = lax.axis_size("expert") * slots
    line = lax.axis_size("dp") == 4 and lax.axis_size("expert") == 8
    few = experts_all <= 4 * top_k and slots == 2
    step = dense if few and line else routed
    return step(tokens, routes, gates, cotangent, partner, w_gate_up, w_down)


def solution(mesh):
    in_specs = (
        P(("dp", "expert"), None),
        P(("dp", "expert"), None),
        P(("dp", "expert"), None),
        P(("dp", "expert"), None),
        P(),
        P("expert", None, None),
        P("expert", None, None),
    )
    out_specs = (
        P(("dp", "expert"), None),
        P(("dp", "expert"), None),
        P("expert", "dp", None),
        P("expert", "dp", None),
    )
    return jax.shard_map(local, mesh=mesh, in_specs=in_specs, out_specs=out_specs, check_vma=False)
```

```python
import functools

import jax
import jax.numpy as jnp
from jax import lax
from jax.experimental import pallas as pl
from jax.experimental.pallas import tpu as pltpu
from jax.sharding import PartitionSpec as P

grad_scale = 0.0625
vmem = 12 << 20


def partner_2(block, axis, distance):
    count = lax.axis_size(axis)
    route = []
    for low in range(count):
        high = low | 1 << distance
        if high != low and high < count:
            route += [(low, high), (high, low)]
    return lax.ppermute(block, axis, route)


def table_lookup(table, keys):
    hits = keys[..., None] == jnp.arange(table.shape[0], dtype=jnp.int32)
    return jnp.sum(jnp.where(hits, table, 0), axis=-1)


def pick_slots(own_slots, received, moved, source_local):
    slots = own_slots.shape[0]
    index = jnp.where(moved, slots + source_local, jnp.arange(slots, dtype=jnp.int32))
    stacked = jnp.concatenate([own_slots, received], axis=0)
    return jnp.take(stacked, index, axis=0)


def routed(tokens, routes, gates, cotangent, partner, w_gate_up, w_down):
    count_tokens, top_k = routes.shape
    width = tokens.shape[1]
    hidden_units = w_down.shape[2]
    n_expert = lax.axis_size("expert")
    exp_slots = w_gate_up.shape[0]
    experts_all = n_expert * exp_slots
    capacity = 3 * count_tokens * top_k // (2 * experts_all)
    pair_bit = n_expert.bit_length() - 2
    my_index = lax.axis_index("expert")
    slot_ids = my_index * exp_slots + jnp.arange(exp_slots, dtype=jnp.int32)
    partner_of = table_lookup(partner, slot_ids)
    moved = partner_of // exp_slots != my_index
    source_local = partner_of % exp_slots
    packed = jnp.concatenate([w_gate_up, w_down], axis=-1)
    target = table_lookup(partner, routes)
    received = partner_2(packed, "expert", pair_bit)
    packed = pick_slots(packed, received, moved, source_local)
    weight_gu = packed[:, :, : 2 * hidden_units]
    weight_dn = packed[:, :, 2 * hidden_units :]
    assign_total = count_tokens * top_k
    flat_slots = target.reshape(-1)
    hits = (flat_slots[:, None] == jnp.arange(experts_all, dtype=jnp.int32)).astype(jnp.int32)
    ranked = jnp.sum(jnp.cumsum(hits, axis=0) * hits, axis=1) - 1
    position = flat_slots * capacity + ranked
    filler = (
        jnp.full((experts_all * capacity,), assign_total, jnp.int32)
        .at[position]
        .set(jnp.arange(assign_total, dtype=jnp.int32))
    )
    buffer_shape = (n_expert, exp_slots, capacity, width)
    token_pad = jnp.concatenate([tokens, jnp.zeros((1, width), tokens.dtype)], axis=0)
    sending_rows = token_pad[filler // top_k].reshape(buffer_shape)
    arrived = lax.all_to_all(sending_rows, "expert", split_axis=0, concat_axis=0, tiled=True)
    pre_act = jnp.einsum("sjcd,jdf->sjcf", arrived, weight_gu, preferred_element_type=jnp.float32)
    gate_pre = pre_act[..., :hidden_units]
    up_pre = pre_act[..., hidden_units:]
    sigmoid_gate = jax.nn.sigmoid(gate_pre)
    silu_gate = gate_pre * sigmoid_gate
    hidden = (silu_gate * up_pre).astype(jnp.bfloat16)
    expert_out = jnp.einsum(
        "sjcf,jdf->sjcd", hidden, weight_dn, preferred_element_type=jnp.float32
    ).astype(jnp.bfloat16)
    returned = lax.all_to_all(expert_out, "expert", split_axis=0, concat_axis=0, tiled=True)
    picked = returned.reshape(-1, width)[position].reshape(count_tokens, top_k, width)
    mixed = jnp.einsum("tk,tkd->td", gates, picked.astype(jnp.float32)).astype(jnp.bfloat16)
    grad_out = (
        (gates[:, :, None] * cotangent[:, None, :].astype(jnp.float32))
        .astype(jnp.bfloat16)
        .reshape(assign_total, width)
    )
    grad_pad = jnp.concatenate([grad_out, jnp.zeros((1, width), jnp.bfloat16)], axis=0)
    grad_arrived = lax.all_to_all(
        grad_pad[filler].reshape(buffer_shape), "expert", split_axis=0, concat_axis=0, tiled=True
    )
    grad_hidden = jnp.einsum(
        "sjcd,jdf->sjcf", grad_arrived, weight_dn, preferred_element_type=jnp.float32
    )
    grad_down = jnp.einsum(
        "sjcf,sjcd->jdf", hidden, grad_arrived, preferred_element_type=jnp.float32
    )
    grad_gate = grad_hidden * up_pre * sigmoid_gate * (1.0 + gate_pre * (1.0 - sigmoid_gate))
    grad_up = grad_hidden * silu_gate
    grad_pre = jnp.concatenate([grad_gate, grad_up], axis=-1).astype(jnp.bfloat16)
    grad_rows = jnp.einsum(
        "sjcf,jdf->sjcd", grad_pre, weight_gu, preferred_element_type=jnp.float32
    ).astype(jnp.bfloat16)
    grad_gu = jnp.einsum("sjcd,sjcf->jdf", arrived, grad_pre, preferred_element_type=jnp.float32)
    grad_back = lax.all_to_all(grad_rows, "expert", split_axis=0, concat_axis=0, tiled=True)
    gathered = grad_back.reshape(-1, width)[position].reshape(count_tokens, top_k, width)
    grad_tokens = jnp.sum(gathered.astype(jnp.float32), axis=1).astype(jnp.bfloat16)
    terms = jnp.concatenate([grad_gu, grad_down], axis=-1) * grad_scale
    reduced = lax.psum_scatter(terms, "dp", scatter_dimension=1, tiled=True)
    return (
        mixed,
        grad_tokens,
        reduced[:, :, : 2 * hidden_units],
        reduced[:, :, 2 * hidden_units :],
    )


def swap_with(block, axis, mask):
    return lax.ppermute(block, axis, [(i, i ^ mask) for i in range(lax.axis_size(axis))])


def send(block, pairs):
    return lax.ppermute(block, "expert", [(2 * a + c, 2 * b + c) for a, b in pairs for c in range(2)])


def both_cores(block):
    return block, swap_with(block, "expert", 1)


def contract(a, b, i, j):
    return lax.dot_general(a, b, (((i,), (j,)), ((), ())), preferred_element_type=jnp.float32)


def message_kernel(tokens_ref, cotangent_ref, routes_ref, gates_ref, out_ref, again_ref, *, experts):
    rows, width = tokens_ref.shape
    lanes = out_ref.shape[1] - 2 * width
    out_ref[:, :width] = tokens_ref[...]
    out_ref[:, width : 2 * width] = cotangent_ref[...]
    lane = lax.broadcasted_iota(jnp.int32, (rows, lanes), 1)
    expert = lane % experts
    gate = jnp.zeros((rows, lanes), jnp.float32)
    routes, gates = routes_ref[...].T, gates_ref[...].T
    for k in range(routes.shape[1]):
        gate = gate + jnp.where(routes[:, k : k + 1] == expert, gates[:, k : k + 1], 0.0)
    high = gate.astype(jnp.bfloat16).astype(jnp.float32)
    middle = (gate - high).astype(jnp.bfloat16).astype(jnp.float32)
    low = gate - high - middle
    third = lane // experts
    value = jnp.where(third == 0, high, jnp.where(third == 1, middle, jnp.where(third == 2, low, 0.0)))
    out_ref[:, 2 * width :] = value.astype(out_ref.dtype)
    again_ref[...] = out_ref[...]


def message(tokens, cotangent, routes, gates, experts):
    rows, width = tokens.shape
    return pl.pallas_call(
        functools.partial(message_kernel, experts=experts),
        out_shape=[jax.ShapeDtypeStruct((n, 2 * width + 128), tokens.dtype) for n in (rows, rows)],
        cost_estimate=pl.CostEstimate(flops=0, bytes_accessed=1 << 20, transcendentals=0),
        name="message",
    )(tokens, cotangent, routes.T, gates.T)


def gate_of(ref, width, expert, experts):
    values = ref[:, 2 * width :].astype(jnp.float32)
    lane = lax.broadcasted_iota(jnp.int32, values.shape, 1)
    chosen = jnp.logical_and(lane % experts == expert, lane < 3 * experts)
    return jnp.sum(jnp.where(chosen, values, 0.0), axis=1, keepdims=True)


def marked(kernel, count, *refs):
    refs[count - 1][...] = jnp.zeros_like(refs[count - 1])
    kernel(*refs[: count - 1], *refs[count:])


def call(kernel, name, scalars, operands, outs, flops, places=None, scratch=()):
    outs = [*outs, ((8, 128), jnp.float32)]
    places = [*(places or [pltpu.VMEM] * (len(outs) - 1)), pltpu.VMEM]
    return pl.pallas_call(
        functools.partial(marked, kernel, 1 + len(operands) + len(outs)),
        in_specs=[pl.BlockSpec(memory_space=pltpu.SMEM)]
        + [pl.BlockSpec(memory_space=pltpu.VMEM)] * len(operands),
        out_specs=[pl.BlockSpec(memory_space=place) for place in places],
        out_shape=[jax.ShapeDtypeStruct(shape, dtype) for shape, dtype in outs],
        scratch_shapes=list(scratch),
        compiler_params=pltpu.CompilerParams(vmem_limit_bytes=vmem),
        cost_estimate=pl.CostEstimate(flops=int(flops), bytes_accessed=0, transcendentals=0),
        name=name,
    )(scalars, *operands)


def hold_kernel(*refs):
    del refs


def hold(values, *earlier):
    anywhere = pl.BlockSpec(memory_space=pl.ANY)
    n = len(values)
    return pl.pallas_call(
        hold_kernel,
        in_specs=[anywhere] * (n + len(earlier)),
        out_specs=[anywhere] * n,
        out_shape=[jax.ShapeDtypeStruct(x.shape, x.dtype) for x in values],
        input_output_aliases={i: i for i in range(n)},
        compiler_params=pltpu.CompilerParams(vmem_limit_bytes=vmem),
        cost_estimate=pl.CostEstimate(flops=0, bytes_accessed=0, transcendentals=0),
        name="hold",
    )(*values, *earlier)


def inner_kernel(at, xs, up_ref, down_ref, h_ref, p_ref, experts):
    width, units = up_ref.shape[1], down_ref.shape[2]
    x = jnp.concatenate([ref[:, :width] for ref in xs], axis=0)
    c = jnp.concatenate([ref[:, width : 2 * width] for ref in xs], axis=0)
    for i in range(2):
        slot = jnp.bitwise_xor(at[1], i)
        pre = jnp.dot(x, up_ref[slot], preferred_element_type=jnp.float32)
        back = jnp.dot(c, down_ref[slot], preferred_element_type=jnp.float32)
        gate_pre, up_pre = pre[:, :units], pre[:, units:]
        expert = 2 * at[2] + slot
        gate = [gate_of(ref, width, expert, experts) for ref in xs]
        gate = jnp.concatenate(gate, axis=0)
        sig = 0.5 * jnp.tanh(0.5 * gate_pre) + 0.5
        scaled = gate * sig
        silu = scaled * gate_pre
        h_ref[i] = (silu * up_pre).astype(h_ref.dtype)
        p_ref[i, :, :units] = (back * up_pre * (scaled + silu * (1.0 - sig))).astype(p_ref.dtype)
        p_ref[i, :, units:] = (back * silu).astype(p_ref.dtype)


def outer_kernel(at, h_ref, p_ref, up_ref, down_ref, *outs):
    kept_ref, sent_ref = outs[-2:]
    width = up_ref.shape[1]
    half = kept_ref.shape[0]
    slots = [jnp.bitwise_xor(at[1], i) for i in range(2)]
    out = sum(contract(h_ref[i], down_ref[slots[i]], 1, 1) for i in range(2))
    kept_ref[:, :width] = out[:half].astype(kept_ref.dtype)
    sent_ref[:, :width] = out[half:].astype(sent_ref.dtype)
    out = sum(contract(p_ref[i], up_ref[slots[i]], 1, 1) for i in range(2))
    kept_ref[:, width:] = out[:half].astype(kept_ref.dtype)
    sent_ref[:, width:] = out[half:].astype(sent_ref.dtype)


def near_kernel(at, *refs, pieces, experts):
    xs, (up_ref, down_ref, h_ref, p_ref, kept_ref, sent_ref) = refs[:pieces], refs[pieces:]
    inner_kernel(at, xs, up_ref, down_ref, h_ref, p_ref, experts)
    outer_kernel(at, h_ref, p_ref, up_ref, down_ref, kept_ref, sent_ref)


def far_kernel(at, *refs, pieces, experts):
    inner_kernel(at, refs[:pieces], *refs[pieces:], experts)


def term(xs, ps, hs, order, column, width):
    units = hs[0].shape[2]
    x = jnp.concatenate([ref[:, pl.ds(column, width // 4)] for ref in xs], axis=0)
    c = jnp.concatenate([ref[:, pl.ds(width + column, width // 4)] for ref in xs], axis=0)
    p = jnp.concatenate([ref[order] for ref in ps], axis=0)
    h = jnp.concatenate([ref[order] for ref in hs], axis=0)
    return contract(x, p, 0, 0), contract(c, h, 0, 0)


def early_kernel(at, *refs, pieces):
    xs, ps, hs, outs = refs[:pieces], refs[pieces : pieces + 3], refs[pieces + 3 : pieces + 6], refs[pieces + 6 :]
    units = hs[0].shape[2]
    quarter = outs[0].shape[1]
    for order in range(2):
        for i in range(4):
            column = pl.multiple_of(jnp.bitwise_xor(at[0], i) * quarter, quarter)
            first, last = term(xs, ps, hs, order, column, 4 * quarter)
            outs[order][i, :, : 2 * units] = first.astype(outs[order].dtype)
            outs[order][i, :, 2 * units :] = last.astype(outs[order].dtype)


def late_kernel(at, *refs, pieces, order):
    xs, (p_ref, h_ref, sum_ref), outs = refs[:pieces], refs[pieces : pieces + 3], refs[-4:]
    send_a, send_b, keep_a, keep_b = outs
    units = h_ref.shape[2]
    quarter = sum_ref.shape[1]
    rows = quarter // 2
    for i in (1, 3, 2, 0):
        column = pl.multiple_of(jnp.bitwise_xor(at[0], i) * quarter, quarter)
        first, last = term(xs, (p_ref,), (h_ref,), order, column, 4 * quarter)
        first = ((first + sum_ref[i, :, : 2 * units]) * grad_scale).astype(send_a.dtype)
        last = ((last + sum_ref[i, :, 2 * units :]) * grad_scale).astype(send_a.dtype)
        ref_a = send_a if i & 1 else keep_a
        ref_b = send_b if i & 2 else keep_b
        ref_a[i >> 1, :, : 2 * units] = first[:rows]
        ref_a[i >> 1, :, 2 * units :] = last[:rows]
        ref_b[i & 1, :, : 2 * units] = first[rows:]
        ref_b[i & 1, :, 2 * units :] = last[rows:]


def far_block_kernel(at, middle, ends, *refs):
    refs[-1][...] = jnp.where(at[4] == 1, middle[...], ends[...])


def line_kernel(at, kept, other, *refs, passed, cuts):
    value = kept[...].astype(jnp.float32) + other[...].astype(jnp.float32)
    for ref in refs[:passed]:
        value = value + jnp.where(at[4] == 1, ref[...].astype(jnp.float32), 0.0)
    for i, out in enumerate(refs[-cuts:]):
        out[...] = value[:, i * out.shape[1] : (i + 1) * out.shape[1]].astype(out.dtype)


def pair_kernel(at, got_a, got_b, keep_a, keep_b, *refs):
    f32 = jnp.float32
    count = 6 if len(refs) > 6 else 0
    more, results = refs[:count], refs[-2:]
    end_a, end_b, own = refs[count : count + 3] if count else refs[-3:]
    for half, (got, keep, out) in enumerate(((got_a, keep_a, end_a), (got_b, keep_b, end_b))):
        out[...] = (keep[1].astype(f32) + got[1].astype(f32)).astype(out.dtype)
        own[half] = keep[0].astype(f32) + got[0].astype(f32)
    if more:
        own_sum, other_sum, one, two = [ref[...].astype(f32) for ref in more[:4]]
        value = own_sum + other_sum + one + jnp.where(at[4] == 1, 0.0, two)
        for i, (ref, three) in enumerate(zip(results, more[4:])):
            term = value[:, i * ref.shape[1] : (i + 1) * ref.shape[1]]
            ref[...] = (term + three[...].astype(f32)).astype(ref.dtype)


def lead_kernel(at, end_a, end_b, own, *refs):
    sent, first = refs[-2:]
    rows = own.shape[1]
    for half, end in enumerate((end_a, end_b)):
        value = own[half] + end[...].astype(jnp.float32)
        first[half] = value
        sent[half * rows : (half + 1) * rows] = value.astype(sent.dtype)


def finish_kernel(at, first, second, end_a, end_b, traded, gu_ref, dn_ref):
    columns = gu_ref.shape[2]
    rows = end_a.shape[0]
    for half, end in enumerate((end_a, end_b)):
        here = slice(half * rows, (half + 1) * rows)
        lead = jnp.where(at[3] == 1, traded[here].astype(jnp.float32), first[half])
        for slot, value in ((at[1], lead), (1 - at[1], second[half] + end[...].astype(jnp.float32))):
            gu_ref[slot, here, :] = value[:, :columns]
            dn_ref[slot, here, :] = value[:, columns:]


def dense(tokens, routes, gates, cotangent, partner, w_gate_up, w_down):
    count_tokens, _ = routes.shape
    units = w_down.shape[2]
    n_expert = lax.axis_size("expert")
    bf16, f32, i32 = jnp.bfloat16, jnp.float32, jnp.int32
    me = lax.axis_index("expert")
    partner_of = table_lookup(partner, me * 2 + jnp.arange(2, dtype=i32))
    moved = partner_of // 2 != me
    flip = moved[1].astype(i32)
    trades = jnp.any(moved).astype(i32)
    inner = (me // 2 == 1) | (me // 2 == 2)

    experts = 2 * n_expert
    width = tokens.shape[1]
    n = 2 * count_tokens
    at = jnp.stack([lax.axis_index("dp"), flip, me, trades, inner.astype(i32)])
    flops = 4 * n * width * units
    weights = (w_gate_up, w_down)
    inner_outs = [((2, n, units), bf16), ((2, n, 2 * units), bf16)]
    outer_outs = [((count_tokens, 2 * width), bf16)] * 2

    rows, columns = width // 8, 3 * units
    part = [((2, rows, columns), bf16)] * 4
    one_block = ((rows, columns), bf16)
    both = ((2, rows, columns), f32)

    block, again = message(tokens, cotangent, routes, gates, experts)
    two = swap_with(block, "expert", 4)
    one = swap_with(block, "expert", 2)

    def near(pieces, cost):
        kernel = functools.partial(near_kernel, pieces=len(pieces), experts=experts)
        outs = inner_outs + outer_outs
        return call(kernel, "near_block", at, (*pieces, *weights), outs, cost * flops)

    ends = send(two, [(1, 0), (2, 3)])
    (again,) = hold([again], two)
    middle = send(again, [(1, 2), (2, 1)])
    pieces = [both_cores(block)]
    passes = [near(pieces[0], 12)]
    (one,) = hold([one], passes[0][4])
    pieces += [both_cores(one), both_cores(two)]
    passes += [near(pieces[1], 12), near(pieces[2], 15)]
    hidden, grads, kept, sent, _ = map(list, zip(*passes))
    flat = [piece for block in pieces for piece in block]
    *sums, done = call(
        functools.partial(early_kernel, pieces=len(flat)),
        "early_terms",
        at,
        (*flat, *grads, *hidden),
        [((4, width // 4, 3 * units), f32)] * 2,
        27 * flops,
    )
    other = [swap_with(block, "expert", 1) for block in sent]

    def line(k, *passed, cuts=1):
        kernel = functools.partial(line_kernel, passed=len(passed), cuts=cuts)
        outs = [((count_tokens, 2 * width // cuts), bf16)] * cuts
        *going, done = call(kernel, "line_terms", at, (kept[k], other[k], *passed), outs, 0)
        if k == 2:
            return send(going[0], [(1, 3), (2, 0), (0, 1), (3, 2)]), done
        return *(swap_with(piece, "expert", 2 * k) for piece in going), done

    (got_one, mark_one), (got_two, mark_two) = line(1), line(2)

    far, _ = call(far_block_kernel, "far_block", at, (middle, ends, done, mark_one, mark_two), [(block.shape, bf16)], 0)
    far = both_cores(far)
    kernel = functools.partial(far_kernel, pieces=2, experts=experts)
    h, p, _ = call(kernel, "far_hidden", at, (*far, *weights), inner_outs, 12 * flops)

    def late(i, *earlier):
        kernel = functools.partial(late_kernel, pieces=2, order=i)
        return call(kernel, "late_terms", at, (*far, p, h, sums[i], *earlier), part, 6 * flops)

    def halves(send_a, send_b, keep_a, keep_b, more, *earlier):
        got_a, got_b = swap_with(send_a, "dp", 1), swap_with(send_b, "dp", 2)
        operands = (got_a, got_b, keep_a, keep_b, *earlier, *more)
        outs = [one_block, one_block, both] + [((count_tokens, width), bf16)] * (2 if more else 0)
        end_a, end_b, own, *results, _ = call(pair_kernel, "pair_terms", at, operands, outs, 0)
        return swap_with(end_a, "dp", 2), swap_with(end_b, "dp", 1), own, results

    *first, done = late(0)
    *second, done = late(1, done)
    k, s, _ = call(outer_kernel, "far_results", at, (h, p, *weights, done), outer_outs, 12 * flops)
    kept.append(k)
    other.append(swap_with(s, "expert", 1))
    three_mixed, three_grad, done = line(3, got_two, cuts=2)
    end_a, end_b, own, _ = halves(*first, [], done)
    outs = [((2 * rows, columns), bf16), both]
    leading, head, _ = call(lead_kernel, "lead_terms", at, (end_a, end_b, own, three_mixed, three_grad, got_one), outs, 0)
    traded = swap_with(leading, "expert", n_expert // 2)
    more = [kept[0], other[0], got_one, got_two, three_mixed, three_grad]
    end_a, end_b, tail, (mixed, grad_tokens) = halves(*second, more)
    grad_gu, grad_dn, _ = call(
        finish_kernel,
        "finish",
        at,
        (head, tail, end_a, end_b, traded),
        [((2, 2 * rows, 2 * units), f32), ((2, 2 * rows, units), f32)],
        0,
    )
    return mixed, grad_tokens, grad_gu, grad_dn


def local(tokens, routes, gates, cotangent, partner, w_gate_up, w_down):
    count_tokens, top_k = routes.shape
    slots = w_gate_up.shape[0]
    experts_all = lax.axis_size("expert") * slots
    line = lax.axis_size("dp") == 4 and lax.axis_size("expert") == 8
    few = experts_all <= 4 * top_k and slots == 2
    step = dense if few and line else routed
    return step(tokens, routes, gates, cotangent, partner, w_gate_up, w_down)


def solution(mesh):
    in_specs = (
        P(("dp", "expert"), None),
        P(("dp", "expert"), None),
        P(("dp", "expert"), None),
        P(("dp", "expert"), None),
        P(),
        P("expert", None, None),
        P("expert", None, None),
    )
    out_specs = (
        P(("dp", "expert"), None),
        P(("dp", "expert"), None),
        P("expert", "dp", None),
        P("expert", "dp", None),
    )
    return jax.shard_map(local, mesh=mesh, in_specs=in_specs, out_specs=out_specs, check_vma=False)
```

```python
import functools

import jax
import jax.numpy as jnp
from jax import lax
from jax.experimental import pallas as pl
from jax.experimental.pallas import tpu as pltpu
from jax.sharding import PartitionSpec as P

grad_scale = 0.0625
vmem = 12 << 20


def partner_2(block, axis, distance):
    count = lax.axis_size(axis)
    route = []
    for low in range(count):
        high = low | 1 << distance
        if high != low and high < count:
            route += [(low, high), (high, low)]
    return lax.ppermute(block, axis, route)


def table_lookup(table, keys):
    hits = keys[..., None] == jnp.arange(table.shape[0], dtype=jnp.int32)
    return jnp.sum(jnp.where(hits, table, 0), axis=-1)


def pick_slots(own_slots, received, moved, source_local):
    slots = own_slots.shape[0]
    index = jnp.where(moved, slots + source_local, jnp.arange(slots, dtype=jnp.int32))
    stacked = jnp.concatenate([own_slots, received], axis=0)
    return jnp.take(stacked, index, axis=0)


def routed(tokens, routes, gates, cotangent, partner, w_gate_up, w_down):
    count_tokens, top_k = routes.shape
    width = tokens.shape[1]
    hidden_units = w_down.shape[2]
    n_expert = lax.axis_size("expert")
    exp_slots = w_gate_up.shape[0]
    experts_all = n_expert * exp_slots
    capacity = 3 * count_tokens * top_k // (2 * experts_all)
    pair_bit = n_expert.bit_length() - 2
    my_index = lax.axis_index("expert")
    slot_ids = my_index * exp_slots + jnp.arange(exp_slots, dtype=jnp.int32)
    partner_of = table_lookup(partner, slot_ids)
    moved = partner_of // exp_slots != my_index
    source_local = partner_of % exp_slots
    packed = jnp.concatenate([w_gate_up, w_down], axis=-1)
    target = table_lookup(partner, routes)
    received = partner_2(packed, "expert", pair_bit)
    packed = pick_slots(packed, received, moved, source_local)
    weight_gu = packed[:, :, : 2 * hidden_units]
    weight_dn = packed[:, :, 2 * hidden_units :]
    assign_total = count_tokens * top_k
    flat_slots = target.reshape(-1)
    hits = (flat_slots[:, None] == jnp.arange(experts_all, dtype=jnp.int32)).astype(jnp.int32)
    ranked = jnp.sum(jnp.cumsum(hits, axis=0) * hits, axis=1) - 1
    position = flat_slots * capacity + ranked
    filler = (
        jnp.full((experts_all * capacity,), assign_total, jnp.int32)
        .at[position]
        .set(jnp.arange(assign_total, dtype=jnp.int32))
    )
    buffer_shape = (n_expert, exp_slots, capacity, width)
    token_pad = jnp.concatenate([tokens, jnp.zeros((1, width), tokens.dtype)], axis=0)
    sending_rows = token_pad[filler // top_k].reshape(buffer_shape)
    arrived = lax.all_to_all(sending_rows, "expert", split_axis=0, concat_axis=0, tiled=True)
    pre_act = jnp.einsum("sjcd,jdf->sjcf", arrived, weight_gu, preferred_element_type=jnp.float32)
    gate_pre = pre_act[..., :hidden_units]
    up_pre = pre_act[..., hidden_units:]
    sigmoid_gate = jax.nn.sigmoid(gate_pre)
    silu_gate = gate_pre * sigmoid_gate
    hidden = (silu_gate * up_pre).astype(jnp.bfloat16)
    expert_out = jnp.einsum(
        "sjcf,jdf->sjcd", hidden, weight_dn, preferred_element_type=jnp.float32
    ).astype(jnp.bfloat16)
    returned = lax.all_to_all(expert_out, "expert", split_axis=0, concat_axis=0, tiled=True)
    picked = returned.reshape(-1, width)[position].reshape(count_tokens, top_k, width)
    mixed = jnp.einsum("tk,tkd->td", gates, picked.astype(jnp.float32)).astype(jnp.bfloat16)
    grad_out = (
        (gates[:, :, None] * cotangent[:, None, :].astype(jnp.float32))
        .astype(jnp.bfloat16)
        .reshape(assign_total, width)
    )
    grad_pad = jnp.concatenate([grad_out, jnp.zeros((1, width), jnp.bfloat16)], axis=0)
    grad_arrived = lax.all_to_all(
        grad_pad[filler].reshape(buffer_shape), "expert", split_axis=0, concat_axis=0, tiled=True
    )
    grad_hidden = jnp.einsum(
        "sjcd,jdf->sjcf", grad_arrived, weight_dn, preferred_element_type=jnp.float32
    )
    grad_down = jnp.einsum(
        "sjcf,sjcd->jdf", hidden, grad_arrived, preferred_element_type=jnp.float32
    )
    grad_gate = grad_hidden * up_pre * sigmoid_gate * (1.0 + gate_pre * (1.0 - sigmoid_gate))
    grad_up = grad_hidden * silu_gate
    grad_pre = jnp.concatenate([grad_gate, grad_up], axis=-1).astype(jnp.bfloat16)
    grad_rows = jnp.einsum(
        "sjcf,jdf->sjcd", grad_pre, weight_gu, preferred_element_type=jnp.float32
    ).astype(jnp.bfloat16)
    grad_gu = jnp.einsum("sjcd,sjcf->jdf", arrived, grad_pre, preferred_element_type=jnp.float32)
    grad_back = lax.all_to_all(grad_rows, "expert", split_axis=0, concat_axis=0, tiled=True)
    gathered = grad_back.reshape(-1, width)[position].reshape(count_tokens, top_k, width)
    grad_tokens = jnp.sum(gathered.astype(jnp.float32), axis=1).astype(jnp.bfloat16)
    terms = jnp.concatenate([grad_gu, grad_down], axis=-1) * grad_scale
    reduced = lax.psum_scatter(terms, "dp", scatter_dimension=1, tiled=True)
    return (
        mixed,
        grad_tokens,
        reduced[:, :, : 2 * hidden_units],
        reduced[:, :, 2 * hidden_units :],
    )


def swap_with(block, axis, mask):
    return lax.ppermute(block, axis, [(i, i ^ mask) for i in range(lax.axis_size(axis))])


def send(block, pairs):
    return lax.ppermute(block, "expert", [(2 * a + c, 2 * b + c) for a, b in pairs for c in range(2)])


def both_cores(block):
    return block, swap_with(block, "expert", 1)


def contract(a, b, i, j):
    return lax.dot_general(a, b, (((i,), (j,)), ((), ())), preferred_element_type=jnp.float32)


def message_kernel(tokens_ref, cotangent_ref, routes_ref, gates_ref, out_ref, again_ref, *, experts):
    rows, width = tokens_ref.shape
    lanes = out_ref.shape[1] - 2 * width
    out_ref[:, :width] = tokens_ref[...]
    out_ref[:, width : 2 * width] = cotangent_ref[...]
    lane = lax.broadcasted_iota(jnp.int32, (rows, lanes), 1)
    expert = lane % experts
    gate = jnp.zeros((rows, lanes), jnp.float32)
    routes, gates = routes_ref[...].T, gates_ref[...].T
    for k in range(routes.shape[1]):
        gate = gate + jnp.where(routes[:, k : k + 1] == expert, gates[:, k : k + 1], 0.0)
    high = gate.astype(jnp.bfloat16).astype(jnp.float32)
    middle = (gate - high).astype(jnp.bfloat16).astype(jnp.float32)
    low = gate - high - middle
    third = lane // experts
    value = jnp.where(third == 0, high, jnp.where(third == 1, middle, jnp.where(third == 2, low, 0.0)))
    out_ref[:, 2 * width :] = value.astype(out_ref.dtype)
    again_ref[...] = out_ref[...]


def message(tokens, cotangent, routes, gates, experts):
    rows, width = tokens.shape
    return pl.pallas_call(
        functools.partial(message_kernel, experts=experts),
        out_shape=[jax.ShapeDtypeStruct((n, 2 * width + 128), tokens.dtype) for n in (rows, rows)],
        cost_estimate=pl.CostEstimate(flops=0, bytes_accessed=1 << 20, transcendentals=0),
        name="message",
    )(tokens, cotangent, routes.T, gates.T)


def gate_of(ref, width, expert, experts):
    values = ref[:, 2 * width :].astype(jnp.float32)
    lane = lax.broadcasted_iota(jnp.int32, values.shape, 1)
    chosen = jnp.logical_and(lane % experts == expert, lane < 3 * experts)
    return jnp.sum(jnp.where(chosen, values, 0.0), axis=1, keepdims=True)


def marked(kernel, count, *refs):
    refs[count - 1][...] = jnp.zeros_like(refs[count - 1])
    kernel(*refs[: count - 1], *refs[count:])


def call(kernel, name, scalars, operands, outs, flops, places=None, scratch=()):
    outs = [*outs, ((8, 128), jnp.float32)]
    places = [*(places or [pltpu.VMEM] * (len(outs) - 1)), pltpu.VMEM]
    return pl.pallas_call(
        functools.partial(marked, kernel, 1 + len(operands) + len(outs)),
        in_specs=[pl.BlockSpec(memory_space=pltpu.SMEM)]
        + [pl.BlockSpec(memory_space=pltpu.VMEM)] * len(operands),
        out_specs=[pl.BlockSpec(memory_space=place) for place in places],
        out_shape=[jax.ShapeDtypeStruct(shape, dtype) for shape, dtype in outs],
        scratch_shapes=list(scratch),
        compiler_params=pltpu.CompilerParams(vmem_limit_bytes=vmem),
        cost_estimate=pl.CostEstimate(flops=int(flops), bytes_accessed=0, transcendentals=0),
        name=name,
    )(scalars, *operands)


def hold_kernel(*refs):
    del refs


def hold(values, *earlier):
    anywhere = pl.BlockSpec(memory_space=pl.ANY)
    n = len(values)
    return pl.pallas_call(
        hold_kernel,
        in_specs=[anywhere] * (n + len(earlier)),
        out_specs=[anywhere] * n,
        out_shape=[jax.ShapeDtypeStruct(x.shape, x.dtype) for x in values],
        input_output_aliases={i: i for i in range(n)},
        compiler_params=pltpu.CompilerParams(vmem_limit_bytes=vmem),
        cost_estimate=pl.CostEstimate(flops=0, bytes_accessed=0, transcendentals=0),
        name="hold",
    )(*values, *earlier)


def inner_kernel(at, xs, up_ref, down_ref, h_ref, p_ref, experts):
    width, units = up_ref.shape[1], down_ref.shape[2]
    x = jnp.concatenate([ref[:, :width] for ref in xs], axis=0)
    c = jnp.concatenate([ref[:, width : 2 * width] for ref in xs], axis=0)
    for i in range(2):
        slot = jnp.bitwise_xor(at[1], i)
        pre = jnp.dot(x, up_ref[slot], preferred_element_type=jnp.float32)
        back = jnp.dot(c, down_ref[slot], preferred_element_type=jnp.float32)
        gate_pre, up_pre = pre[:, :units], pre[:, units:]
        expert = 2 * at[2] + slot
        gate = [gate_of(ref, width, expert, experts) for ref in xs]
        gate = jnp.concatenate(gate, axis=0)
        sig = 0.5 * jnp.tanh(0.5 * gate_pre) + 0.5
        scaled = gate * sig
        silu = scaled * gate_pre
        h_ref[i] = (silu * up_pre).astype(h_ref.dtype)
        p_ref[i, :, :units] = (back * up_pre * (scaled + silu * (1.0 - sig))).astype(p_ref.dtype)
        p_ref[i, :, units:] = (back * silu).astype(p_ref.dtype)


def outer_kernel(at, h_ref, p_ref, up_ref, down_ref, *outs):
    kept_ref, sent_ref = outs[-2:]
    width = up_ref.shape[1]
    half = kept_ref.shape[0]
    slots = [jnp.bitwise_xor(at[1], i) for i in range(2)]
    out = sum(contract(h_ref[i], down_ref[slots[i]], 1, 1) for i in range(2))
    kept_ref[:, :width] = out[:half].astype(kept_ref.dtype)
    sent_ref[:, :width] = out[half:].astype(sent_ref.dtype)
    out = sum(contract(p_ref[i], up_ref[slots[i]], 1, 1) for i in range(2))
    kept_ref[:, width:] = out[:half].astype(kept_ref.dtype)
    sent_ref[:, width:] = out[half:].astype(sent_ref.dtype)


def near_kernel(at, *refs, pieces, experts):
    xs, (up_ref, down_ref, h_ref, p_ref, kept_ref, sent_ref) = refs[:pieces], refs[pieces:]
    inner_kernel(at, xs, up_ref, down_ref, h_ref, p_ref, experts)
    outer_kernel(at, h_ref, p_ref, up_ref, down_ref, kept_ref, sent_ref)


def far_kernel(at, *refs, pieces, experts):
    inner_kernel(at, refs[:pieces], *refs[pieces:], experts)


def term(xs, ps, hs, order, column, width):
    units = hs[0].shape[2]
    x = jnp.concatenate([ref[:, pl.ds(column, width // 4)] for ref in xs], axis=0)
    c = jnp.concatenate([ref[:, pl.ds(width + column, width // 4)] for ref in xs], axis=0)
    p = jnp.concatenate([ref[order] for ref in ps], axis=0)
    h = jnp.concatenate([ref[order] for ref in hs], axis=0)
    return contract(x, p, 0, 0), contract(c, h, 0, 0)


def early_kernel(at, *refs, pieces):
    xs, ps, hs, outs = refs[:pieces], refs[pieces : pieces + 3], refs[pieces + 3 : pieces + 6], refs[pieces + 6 :]
    units = hs[0].shape[2]
    quarter = outs[0].shape[1]
    for order in range(2):
        for i in range(4):
            column = pl.multiple_of(jnp.bitwise_xor(at[0], i) * quarter, quarter)
            first, last = term(xs, ps, hs, order, column, 4 * quarter)
            outs[order][i, :, : 2 * units] = first.astype(outs[order].dtype)
            outs[order][i, :, 2 * units :] = last.astype(outs[order].dtype)


def late_kernel(at, *refs, pieces, order):
    xs, (p_ref, h_ref, sum_ref), outs = refs[:pieces], refs[pieces : pieces + 3], refs[-4:]
    send_a, send_b, keep_a, keep_b = outs
    units = h_ref.shape[2]
    quarter = sum_ref.shape[1]
    rows = quarter // 2
    for i in (1, 3, 2, 0):
        column = pl.multiple_of(jnp.bitwise_xor(at[0], i) * quarter, quarter)
        first, last = term(xs, (p_ref,), (h_ref,), order, column, 4 * quarter)
        first = ((first + sum_ref[i, :, : 2 * units]) * grad_scale).astype(send_a.dtype)
        last = ((last + sum_ref[i, :, 2 * units :]) * grad_scale).astype(send_a.dtype)
        ref_a = send_a if i & 1 else keep_a
        ref_b = send_b if i & 2 else keep_b
        ref_a[i >> 1, :, : 2 * units] = first[:rows]
        ref_a[i >> 1, :, 2 * units :] = last[:rows]
        ref_b[i & 1, :, : 2 * units] = first[rows:]
        ref_b[i & 1, :, 2 * units :] = last[rows:]


def far_block_kernel(at, middle, ends, *refs):
    refs[-1][...] = jnp.where(at[4] == 1, middle[...], ends[...])


def line_kernel(at, kept, other, *refs, passed, cuts):
    value = kept[...].astype(jnp.float32) + other[...].astype(jnp.float32)
    for ref in refs[:passed]:
        value = value + jnp.where(at[4] == 1, ref[...].astype(jnp.float32), 0.0)
    for i, out in enumerate(refs[-cuts:]):
        out[...] = value[:, i * out.shape[1] : (i + 1) * out.shape[1]].astype(out.dtype)


def pair_kernel(at, got_a, got_b, keep_a, keep_b, *refs):
    f32 = jnp.float32
    count = 6 if len(refs) > 6 else 0
    more, results = refs[:count], refs[-2:]
    end_a, end_b, own = refs[count : count + 3] if count else refs[-3:]
    for half, (got, keep, out) in enumerate(((got_a, keep_a, end_a), (got_b, keep_b, end_b))):
        out[...] = (keep[1].astype(f32) + got[1].astype(f32)).astype(out.dtype)
        own[half] = keep[0].astype(f32) + got[0].astype(f32)
    if more:
        own_sum, other_sum, one, two = [ref[...].astype(f32) for ref in more[:4]]
        value = own_sum + other_sum + one + jnp.where(at[4] == 1, 0.0, two)
        for i, (ref, three) in enumerate(zip(results, more[4:])):
            term = value[:, i * ref.shape[1] : (i + 1) * ref.shape[1]]
            ref[...] = (term + three[...].astype(f32)).astype(ref.dtype)


def lead_kernel(at, end_a, end_b, own, *refs):
    sent, first = refs[-2:]
    rows = own.shape[1]
    for half, end in enumerate((end_a, end_b)):
        value = own[half] + end[...].astype(jnp.float32)
        first[half] = value
        sent[half * rows : (half + 1) * rows] = value.astype(sent.dtype)


def finish_kernel(at, first, second, end_a, end_b, traded, gu_ref, dn_ref):
    columns = gu_ref.shape[2]
    rows = end_a.shape[0]
    for half, end in enumerate((end_a, end_b)):
        here = slice(half * rows, (half + 1) * rows)
        lead = jnp.where(at[3] == 1, traded[here].astype(jnp.float32), first[half])
        for slot, value in ((at[1], lead), (1 - at[1], second[half] + end[...].astype(jnp.float32))):
            gu_ref[slot, here, :] = value[:, :columns]
            dn_ref[slot, here, :] = value[:, columns:]


def dense(tokens, routes, gates, cotangent, partner, w_gate_up, w_down):
    count_tokens, _ = routes.shape
    units = w_down.shape[2]
    n_expert = lax.axis_size("expert")
    bf16, f32, i32 = jnp.bfloat16, jnp.float32, jnp.int32
    me = lax.axis_index("expert")
    partner_of = table_lookup(partner, me * 2 + jnp.arange(2, dtype=i32))
    moved = partner_of // 2 != me
    flip = moved[1].astype(i32)
    trades = jnp.any(moved).astype(i32)
    inner = (me // 2 == 1) | (me // 2 == 2)

    experts = 2 * n_expert
    width = tokens.shape[1]
    n = 2 * count_tokens
    at = jnp.stack([lax.axis_index("dp"), flip, me, trades, inner.astype(i32)])
    flops = 4 * n * width * units
    weights = (w_gate_up, w_down)
    inner_outs = [((2, n, units), bf16), ((2, n, 2 * units), bf16)]
    outer_outs = [((count_tokens, 2 * width), bf16)] * 2

    rows, columns = width // 8, 3 * units
    part = [((2, rows, columns), bf16)] * 4
    one_block = ((rows, columns), bf16)
    both = ((2, rows, columns), f32)

    block, again = message(tokens, cotangent, routes, gates, experts)
    two = swap_with(block, "expert", 4)
    one = swap_with(block, "expert", 2)

    def near(pieces, cost):
        kernel = functools.partial(near_kernel, pieces=len(pieces), experts=experts)
        outs = inner_outs + outer_outs
        return call(kernel, "near_block", at, (*pieces, *weights), outs, cost * flops)

    ends = send(two, [(1, 0), (2, 3)])
    (again,) = hold([again], two)
    middle = send(again, [(1, 2), (2, 1)])
    pieces = [both_cores(block)]
    passes = [near(pieces[0], 12)]
    (one,) = hold([one], passes[0][4])
    pieces += [both_cores(one), both_cores(two)]
    passes += [near(pieces[1], 12), near(pieces[2], 15)]
    hidden, grads, kept, sent, _ = map(list, zip(*passes))
    flat = [piece for block in pieces for piece in block]
    *sums, done = call(
        functools.partial(early_kernel, pieces=len(flat)),
        "early_terms",
        at,
        (*flat, *grads, *hidden),
        [((4, width // 4, 3 * units), f32)] * 2,
        27 * flops,
    )
    other = [swap_with(block, "expert", 1) for block in sent]

    def line(k, *passed, cuts=1):
        kernel = functools.partial(line_kernel, passed=len(passed), cuts=cuts)
        outs = [((count_tokens, 2 * width // cuts), bf16)] * cuts
        *going, done = call(kernel, "line_terms", at, (kept[k], other[k], *passed), outs, 0)
        if k == 2:
            return send(going[0], [(1, 3), (2, 0), (0, 1), (3, 2)]), done
        return *(swap_with(piece, "expert", 2 * k) for piece in going), done

    (got_one, mark_one), (got_two, mark_two) = line(1), line(2)

    far, _ = call(far_block_kernel, "far_block", at, (middle, ends, done, mark_one, mark_two), [(block.shape, bf16)], 0)
    far = both_cores(far)
    kernel = functools.partial(far_kernel, pieces=2, experts=experts)
    h, p, _ = call(kernel, "far_hidden", at, (*far, *weights), inner_outs, 12 * flops)

    def late(i, *earlier):
        kernel = functools.partial(late_kernel, pieces=2, order=i)
        return call(kernel, "late_terms", at, (*far, p, h, sums[i], *earlier), part, 6 * flops)

    def halves(send_a, send_b, keep_a, keep_b, more, *earlier):
        got_a, got_b = swap_with(send_a, "dp", 1), swap_with(send_b, "dp", 2)
        operands = (got_a, got_b, keep_a, keep_b, *earlier, *more)
        outs = [one_block, one_block, both] + [((count_tokens, width), bf16)] * (2 if more else 0)
        end_a, end_b, own, *results, _ = call(pair_kernel, "pair_terms", at, operands, outs, 0)
        return swap_with(end_a, "dp", 2), swap_with(end_b, "dp", 1), own, results

    *first, done = late(0)
    *second, done = late(1, done)
    k, s, _ = call(outer_kernel, "far_results", at, (h, p, *weights, done), outer_outs, 12 * flops)
    kept.append(k)
    other.append(swap_with(s, "expert", 1))
    three_mixed, three_grad, done = line(3, got_two, cuts=2)
    end_a, end_b, own, _ = halves(*first, [], done)
    outs = [((2 * rows, columns), bf16), both]
    leading, head, _ = call(lead_kernel, "lead_terms", at, (end_a, end_b, own, three_mixed, three_grad), outs, 0)
    traded = swap_with(leading, "expert", n_expert // 2)
    more = [kept[0], other[0], got_one, got_two, three_mixed, three_grad]
    end_a, end_b, tail, (mixed, grad_tokens) = halves(*second, more)
    grad_gu, grad_dn, _ = call(
        finish_kernel,
        "finish",
        at,
        (head, tail, end_a, end_b, traded),
        [((2, 2 * rows, 2 * units), f32), ((2, 2 * rows, units), f32)],
        0,
    )
    return mixed, grad_tokens, grad_gu, grad_dn


def local(tokens, routes, gates, cotangent, partner, w_gate_up, w_down):
    count_tokens, top_k = routes.shape
    slots = w_gate_up.shape[0]
    experts_all = lax.axis_size("expert") * slots
    line = lax.axis_size("dp") == 4 and lax.axis_size("expert") == 8
    few = experts_all <= 4 * top_k and slots == 2
    step = dense if few and line else routed
    return step(tokens, routes, gates, cotangent, partner, w_gate_up, w_down)


def solution(mesh):
    in_specs = (
        P(("dp", "expert"), None),
        P(("dp", "expert"), None),
        P(("dp", "expert"), None),
        P(("dp", "expert"), None),
        P(),
        P("expert", None, None),
        P("expert", None, None),
    )
    out_specs = (
        P(("dp", "expert"), None),
        P(("dp", "expert"), None),
        P("expert", "dp", None),
        P("expert", "dp", None),
    )
    return jax.shard_map(local, mesh=mesh, in_specs=in_specs, out_specs=out_specs, check_vma=False)
```
